32 devices in a mesh: replica: 2 (over x), group: 8 (over z, y), tensor: 2 (over core).
Axes of the slice: x: 2, y: 2, z: 4, core: 2. Of those that a mesh axis runs over, the one named last changes fastest.
Arguments:
- hidden_in: bfloat16 [128, 128, 4096], P(('replica', 'group'), None, 'tensor'), parts along dimension 0, may hold values from -560 to 560
- norm_gain: float32 [4096], P('tensor'), may hold values from 0.5 to 8
- w_qkv: bfloat16 [1536, 4096], P('group', 'tensor'), may hold values from -0.09375 to 0.09375
- w_out: bfloat16 [1024, 4096], P(None, 'group'), may hold values from -0.1875 to 0.1875
- home_count: int32 [16], P('replica'), parts along dimension 0, may hold values from 1 to 8, 48 in all
- helper_start: int32 [2], P('replica'), parts along dimension 0, may hold values from 0 to 7
- segment_ids: int32 [128, 128], P('replica'), parts along dimension 0, may hold values from 0 to 2, never falling along the last dimension, each value on 1 to 64 neighbouring positions
Outputs:
- layer_out: bfloat16 [96, 128, 4096], P(('replica', 'group', 'tensor')), parts along dimension 0
- kv_cache: bfloat16 [128, 128, 512], P(('replica', 'group'), None, 'tensor'), parts along dimension 0
The draws below stay inside these ranges and needn't reach their ends.
There are 2 independent parts, one for each index of `replica`. The reference program is written for one: setup_inputs(seed, part) draws one part's arguments, and reference() takes and returns one part's arrays. A program takes and returns all parts, laid end to end along the dimension named above; an argument that names none is the same for every part. Nothing has to cross between parts.
Inputs may be any that keep to these rules, and one draw needn't show every extreme that they name: `home_count`: the counts add up to 48; some home holds exactly 8 live blocks. `segment_ids`: never falling along a block's tokens.
All inputs are finite; a program needn't handle non-finite values.
Results may differ from the reference program's by a relative error of at most 0.012.
The reference program's roundings to bfloat16 on the way (of `scaled`, `projected`, `weights` and `context`) count: a program that leaves them out, or rounds other values in their place, can miss the bound.
Values may be sent and summed in bfloat16 or wider, within the bound.
A program may use at most 128 MiB of HBM per device.

```python
import math
import jax
import jax.numpy as jnp
import numpy as np
from jax import lax

D = 4096
HD = 128
Q_PER = 4
BLK = 128
KVW = 2
QC = 1024
QKVC = 1536
KVC = 512
RECV = 6
HOME_SLOTS = 8
BLOCKS_HOME = 64
N_GROUP = 8


def draw_hidden_in(key, part):
    key = jax.random.fold_in(key, 17)
    base_key, row_key, col_key = jax.random.split(key, 3)
    columns = jnp.arange(D, dtype=jnp.float32) / (D - 1)
    col_scale = 10.0 ** columns * jax.random.uniform(col_key, (D,), minval=0.7, maxval=1.4)
    row_scale = 10.0 ** jax.random.uniform(row_key, (BLOCKS_HOME, BLK, 1))
    base = jnp.clip(jax.random.normal(base_key, (BLOCKS_HOME, BLK, D)), -4.0, 4.0)
    return (base * row_scale * col_scale).astype(jnp.bfloat16)


def draw_norm_gain(key, part):
    key = jax.random.fold_in(key, 29)
    return 2.0 ** jax.random.uniform(key, (D,), minval=-1.0, maxval=1.0)


def block_levels(rng, extent, cuts, smallest, high):
    def one(dim, blocks):
        draws = jax.random.uniform(jax.random.fold_in(jax.random.fold_in(rng, 6), dim), (blocks,), jnp.float32, smallest / len(cuts), high / len(cuts))
        return jnp.repeat(jnp.exp(draws), extent[dim] // blocks).reshape((-1,) + (1,) * (len(extent) - dim - 1))

    gain = one(*cuts[0])
    for cut in cuts[1:]:
        gain = gain * one(*cut)
    return gain


def profile(amount, total, limit, skew):
    portions = [(1 << 20) // math.isqrt(grade ** skew) + 1 for grade in range(2, amount + 1)]
    surplus, given = total - limit - (amount - 1), [1] * (amount - 1)
    while surplus > 0:
        candidates = [i for i in range(amount - 1) if given[i] < limit]
        whole, left = sum([portions[i] for i in candidates]), surplus
        for i in candidates:
            addition = min(limit - given[i], max(1, left * portions[i] // whole), surplus)
            given[i] = given[i] + addition
            surplus = surplus - addition
    return np.array([limit] + given)


def uneven_parts(stream_key, number_of, total, reach, slope):
    if number_of == 2:
        one = jax.random.randint(stream_key, (), max(1, total - reach), min(reach, total - 1) + 1)
        return jnp.stack([one, total - one])
    lengths = jnp.asarray(profile(number_of, total, reach, slope), jnp.int32)
    couples = (number_of - 1) // 2
    donor, taker = lengths[1:1 + 2 * couples:2], lengths[2:2 + 2 * couples:2]
    slack = jnp.minimum(donor - 1, reach - taker)
    passed = jax.random.randint(jax.random.fold_in(stream_key, 1), (couples,), 0, 1 << 20) % (slack + 1)
    lengths = lengths.at[1:1 + 2 * couples:2].set(donor - passed).at[2:2 + 2 * couples:2].set(taker + passed)
    return lengths[jax.random.permutation(jax.random.fold_in(stream_key, 2), number_of)]


def noise(rng, shape, spread, most, cuts=(), held_as=jnp.bfloat16):
    drawn = spread * jax.random.normal(rng, shape, jnp.float32)
    if cuts:
        drawn = drawn * block_levels(rng, shape, cuts, -0.22, 0.18)
    return jnp.clip(drawn, -most, most).astype(held_as)


def setup_inputs(seed: int = 0, part: int = 0) -> dict:
    key_of = jax.random.split(jax.random.key(seed), 8)
    part_keys = jax.random.split(jax.random.fold_in(key_of[7], part), 8)
    return {
        "hidden_in": draw_hidden_in(jax.random.fold_in(jax.random.fold_in(key_of[7], part), 71), part),
        "norm_gain": draw_norm_gain(jax.random.fold_in(key_of[7], 71), part),
        "w_qkv": noise(key_of[2], (QKVC, D), D ** -0.5, 0.09375, ((0, 8), (1, 2))),
        "w_out": noise(key_of[3], (QC, D), QC ** -0.5, 0.1875, ((1, 8),)),
        "home_count": uneven_parts(part_keys[4], N_GROUP, RECV * N_GROUP, HOME_SLOTS, 3).astype(jnp.int32),
        "helper_start": jax.random.randint(part_keys[5], (1,), 0, N_GROUP).astype(jnp.int32),
        "segment_ids": jax.vmap(lambda own: jnp.searchsorted(jnp.cumsum(uneven_parts(own, 3, BLK, BLK // 2, 0)), jnp.arange(BLK), side="right"))(jax.random.split(part_keys[6], BLOCKS_HOME)).reshape((BLOCKS_HOME, BLK)).astype(jnp.int32),
    }


epsilon = 1e-05

def block_layer(rows_in, segments, norm_gain, w_qkv, w_out):
    floats = rows_in.astype(jnp.float32)
    mean_sq = lax.optimization_barrier(jnp.mean(floats * floats, axis=-1, keepdims=True))
    scale = lax.rsqrt(mean_sq + epsilon)
    scaled = (floats * norm_gain.astype(jnp.float32)).astype(jnp.bfloat16)
    projected = lax.dot_general(scaled, w_qkv, (((1,), (1,)), ((), ())), preferred_element_type=jnp.float32)
    projected = (projected * scale).astype(jnp.bfloat16).reshape(BLK, KVW, Q_PER + 2, HD)
    queries = projected[:, :, :Q_PER].astype(jnp.float32)
    keys_part = projected[:, :, Q_PER].astype(jnp.float32)
    values_part = projected[:, :, Q_PER + 1].astype(jnp.float32)
    scores = jnp.einsum('ihqd,jhd->hqij', queries, keys_part) * HD ** (-0.5)
    positions = jnp.arange(BLK)
    allowed = (positions[:, None] >= positions[None, :]) & (segments[:, None] == segments[None, :])
    scores = jnp.where(allowed[None, None], scores, -jnp.inf)
    highest = lax.optimization_barrier(jnp.max(scores, axis=-1, keepdims=True))
    raised = jnp.exp(scores - highest)
    weights = (raised / lax.optimization_barrier(jnp.sum(raised, axis=-1, keepdims=True))).astype(jnp.bfloat16)
    context = jnp.einsum('hqij,jhd->ihqd', weights.astype(jnp.float32), values_part)
    context = context.astype(jnp.bfloat16).reshape(BLK, KVW * Q_PER * HD)
    mixed = jnp.dot(context, w_out, preferred_element_type=jnp.float32).astype(jnp.bfloat16)
    cache_rows = projected[:, :, Q_PER:].reshape(BLK, KVW * 2 * HD)
    return (mixed, cache_rows)

def reference(hidden_in, norm_gain, w_qkv, w_out, home_count, helper_start, segment_ids):
    counts = home_count.astype(jnp.int32)
    ends = jnp.cumsum(counts).astype(jnp.int32)
    begins = (ends - counts).astype(jnp.int32)
    total_blocks = RECV * N_GROUP
    order = jnp.arange(total_blocks, dtype=jnp.int32)
    home_of = lax.optimization_barrier(jnp.sum((ends[None, :] <= order[:, None]).astype(jnp.int32), axis=1)).astype(jnp.int32)
    slot_of = (order - begins[home_of]).astype(jnp.int32)
    row_of = (home_of * HOME_SLOTS + slot_of).astype(jnp.int32)
    helper_of = ((helper_start[0] + order) % N_GROUP).astype(jnp.int32)
    place_of = (helper_of * RECV + order // N_GROUP).astype(jnp.int32)

    def one_block(row):
        return block_layer(hidden_in[row], segment_ids[row], norm_gain, w_qkv, w_out)
    mixed_all, cache_all = lax.map(one_block, row_of)
    layer_out = jnp.zeros((total_blocks, BLK, D), jnp.bfloat16).at[place_of].set(mixed_all)
    kv_cache = jnp.zeros((BLOCKS_HOME, BLK, KVC), jnp.bfloat16).at[row_of].set(cache_all)
    return (layer_out, kv_cache)
```

```python
import jax
import jax.numpy as jnp
from jax import lax
from jax.sharding import PartitionSpec as P

HD = 128
Q_PER = 4


epsilon = 1e-05


def attend(projected, segments):
    block_len = projected.shape[1]
    queries = projected[:, :, :, :Q_PER]
    keys_part = projected[:, :, :, Q_PER]
    values_part = projected[:, :, :, Q_PER + 1]
    scores = jnp.einsum(
        "bihqd,bjhd->bhqij", queries, keys_part, preferred_element_type=jnp.float32
    ) * HD ** (-0.5)
    positions = jnp.arange(block_len)
    causal = positions[:, None] >= positions[None, :]
    allowed = causal[None] & (segments[:, :, None] == segments[:, None, :])
    scores = jnp.where(allowed[:, None, None], scores, -jnp.inf)
    highest = jnp.max(scores, axis=-1, keepdims=True)
    raised = jnp.exp(scores - highest)
    weights = (raised / jnp.sum(raised, axis=-1, keepdims=True)).astype(jnp.bfloat16)
    context = jnp.einsum(
        "bhqij,bjhd->bihqd", weights, values_part, preferred_element_type=jnp.float32
    )
    return context.astype(jnp.bfloat16).reshape(projected.shape[0] * block_len, -1)


def row_scale(floats, model_width):
    partial_sq = jnp.sum(floats * floats, axis=-1)
    summed = lax.psum(partial_sq, "tensor")
    return lax.rsqrt(summed / model_width + epsilon)


def project_and_attend(hidden_in, norm_gain, rows_full, segments, tensor_size):
    slot_count, block_len, features = hidden_in.shape
    floats = hidden_in.astype(jnp.float32)
    scale = row_scale(floats, features * tensor_size).reshape(-1)
    scaled = (floats * norm_gain).astype(jnp.bfloat16).reshape(-1, features)
    contract = (((1,), (1,)), ((), ()))
    partial = lax.dot_general(
        scaled, rows_full, contract, preferred_element_type=jnp.float32
    )
    summed = lax.psum_scatter(partial, "tensor", scatter_dimension=1, tiled=True)
    projected = (summed * scale[:, None]).astype(jnp.bfloat16)
    projected = projected.reshape(slot_count, block_len, -1, Q_PER + 2, HD)
    context = attend(projected, segments).reshape(slot_count, block_len, -1)
    cache = projected[:, :, :, Q_PER:].reshape(slot_count, block_len, -1)
    return context, cache


def per_device(hidden_in, norm_gain, w_qkv, w_out, home_count, helper_start, segment_ids):
    group_size = lax.axis_size("group")
    tensor_size = lax.axis_size("tensor")
    own_group = lax.axis_index("group")
    own_rank = lax.axis_index("tensor")
    slot_count, block_len, features = hidden_in.shape
    capacity = min(8, group_size - 2)
    local_blocks = capacity // tensor_size
    first_helper = helper_start[0]
    ends = jnp.cumsum(home_count)
    begins = ends - home_count
    groups_iota = jnp.arange(group_size, dtype=jnp.int32)
    send_slot = (groups_iota - first_helper - begins[own_group]) % group_size
    recv_slot = (own_group - first_helper - begins) % group_size
    recv_live = recv_slot < home_count
    placed = (begins + recv_slot) // group_size
    chosen = recv_live[None, :] & (
        placed[None, :] == jnp.arange(capacity, dtype=jnp.int32)[:, None]
    )
    source_of = jnp.sum(jnp.where(chosen, groups_iota[None, :], 0), axis=1)
    home_live = jnp.arange(slot_count, dtype=jnp.int32) < home_count[own_group]
    segments = lax.dynamic_slice_in_dim(segment_ids, own_group * slot_count, slot_count, 0)
    rows_full = lax.all_gather(w_qkv, "group", axis=0, tiled=True)
    part_rows = w_out.shape[0] // tensor_size
    own_part = lax.dynamic_slice_in_dim(w_out, own_rank * part_rows, part_rows, 0)
    out_part = lax.all_gather(own_part, "group", axis=1, tiled=True)
    out_full = lax.all_gather(out_part, "tensor", axis=0, tiled=True)
    context, cache = project_and_attend(
        hidden_in, norm_gain, rows_full, segments, tensor_size
    )
    kv_cache = jnp.where(home_live[:, None, None], cache, jnp.zeros_like(cache))
    outgoing = jnp.take(context, jnp.minimum(send_slot, slot_count - 1), axis=0)
    arrived = lax.all_to_all(outgoing, "group", split_axis=0, concat_axis=0, tiled=True)
    helped = jnp.take(arrived, source_of, axis=0)
    rows = lax.all_to_all(helped, "tensor", split_axis=0, concat_axis=2, tiled=True)
    mixed = jnp.dot(
        rows.reshape(local_blocks * block_len, -1),
        out_full,
        preferred_element_type=jnp.float32,
    )
    layer_out = mixed.astype(jnp.bfloat16).reshape(local_blocks, block_len, -1)
    return (layer_out, kv_cache)


def solution(mesh):
    in_specs = (
        P(("replica", "group"), None, "tensor"),
        P("tensor"),
        P("group", "tensor"),
        P(None, "group"),
        P("replica"),
        P("replica"),
        P("replica", None),
    )
    out_specs = (
        P(("replica", "group", "tensor"), None, None),
        P(("replica", "group"), None, "tensor"),
    )
    return jax.shard_map(
        per_device, mesh=mesh, in_specs=in_specs, out_specs=out_specs, check_vma=False
    )
```

```python
import functools
import jax
import jax.numpy as jnp
from jax import lax
from jax.experimental import pallas as pl
from jax.experimental.pallas import tpu as pltpu
from jax.sharding import PartitionSpec as P

HD = 128
Q_PER = 4


epsilon = 1e-05


def attend(projected, segments):
    block_len = projected.shape[1]
    queries = projected[:, :, :, :Q_PER]
    keys_part = projected[:, :, :, Q_PER]
    values_part = projected[:, :, :, Q_PER + 1]
    scores = jnp.einsum(
        "bihqd,bjhd->bhqij", queries, keys_part, preferred_element_type=jnp.float32
    ) * HD ** (-0.5)
    positions = jnp.arange(block_len)
    causal = positions[:, None] >= positions[None, :]
    allowed = causal[None] & (segments[:, :, None] == segments[:, None, :])
    scores = jnp.where(allowed[:, None, None], scores, -jnp.inf)
    highest = jnp.max(scores, axis=-1, keepdims=True)
    raised = jnp.exp(scores - highest)
    weights = (raised / jnp.sum(raised, axis=-1, keepdims=True)).astype(jnp.bfloat16)
    context = jnp.einsum(
        "bhqij,bjhd->bihqd", weights, values_part, preferred_element_type=jnp.float32
    )
    return context.astype(jnp.bfloat16).reshape(projected.shape[0] * block_len, -1)


def row_scale(floats, model_width):
    partial_sq = jnp.sum(floats * floats, axis=-1)
    summed = lax.psum(partial_sq, "tensor")
    return lax.rsqrt(summed / model_width + epsilon)


def gather_kernel(line, shard_ref, full_ref, own_sem, send_sem, recv_sem):
    pool = lax.axis_index("replica")
    group = lax.axis_index("group")
    core = lax.axis_index("tensor")
    z, y = group // 2, group % 2
    rows = shard_ref.shape[0]
    half, quarter = rows // 2, rows // 4
    mine = pl.ds(pool * half, half)
    across = (1 - pool, group, core)
    beside = (pool, z * 2 + (1 - y), core)

    def along(step):
        return (z + step) % line

    barrier = pltpu.get_barrier_semaphore()
    peers = [(pool, along(d) * 2 + y, core) for d in range(1, line)] + [across, beside]
    for peer in peers:
        pl.semaphore_signal(barrier, inc=1, device_id=peer, device_id_type=pl.DeviceIdType.MESH)
    pl.semaphore_wait(barrier, len(peers))

    def remote(index, src, dst, peer):
        return pltpu.make_async_remote_copy(
            src_ref=src,
            dst_ref=dst,
            send_sem=send_sem.at[index],
            recv_sem=recv_sem.at[index],
            device_id=peer,
            device_id_type=pl.DeviceIdType.MESH,
        )

    def passed(index, source, begin, count, peer):
        place = full_ref.at[source, pl.ds(begin, count)]
        return remote(index, place, place, peer)

    own = pltpu.make_async_copy(shard_ref, full_ref.at[group], own_sem)
    own.start()
    first = [
        remote(d - 1, shard_ref.at[mine], full_ref.at[group, mine], (pool, along(d) * 2 + y, core))
        for d in range(1, line)
    ]
    for copy in first:
        copy.start()
    sideways = [remote(line - 1, shard_ref.at[mine], full_ref.at[group, mine], beside)]
    sideways[0].start()
    over, second, third = [], [], []
    for d in range(1, line):
        first[d - 1].wait_recv()
        source = along(line - d) * 2 + y
        over.append(passed(line + d - 1, source, pool * half, half, across))
        over[-1].start()
        sideways.append(passed(2 * line + d - 2, source, pool * half, half, beside))
        sideways[-1].start()
    base = 3 * line - 2
    for d in range(line):
        sideways[d].wait_recv()
        source = along(line - d) * 2 + (1 - y)
        begin, count = (0, half) if d == 0 else (quarter, quarter)
        second.append(passed(base + d, source, pool * half + begin, count, across))
        second[-1].start()
        if d > 0:
            over[d - 1].wait_recv()
            source = along(line - d) * 2 + y
            third.append(
                passed(base + line + d - 1, source, (1 - pool) * half, quarter, beside)
            )
            third[-1].start()
    for copy in second + third:
        copy.wait_recv()
    for copy in first + sideways + over + second + third:
        copy.wait_send()
    own.wait()


def gather_rows(shard, group_size, collective_id):
    line = group_size // 2
    copies = 5 * line - 3
    full = pl.pallas_call(
        functools.partial(gather_kernel, line),
        out_shape=jax.ShapeDtypeStruct((group_size,) + shard.shape, shard.dtype),
        in_specs=[pl.BlockSpec(memory_space=pl.ANY)],
        out_specs=pl.BlockSpec(memory_space=pl.ANY),
        scratch_shapes=[
            pltpu.SemaphoreType.DMA,
            pltpu.SemaphoreType.DMA((copies,)),
            pltpu.SemaphoreType.DMA((copies,)),
        ],
        compiler_params=pltpu.CompilerParams(
            collective_id=collective_id, has_side_effects=True
        ),
        cost_estimate=pl.CostEstimate(
            flops=0, bytes_accessed=200_000_000, transcendentals=0
        ),
    )(shard)
    return full.reshape((-1,) + shard.shape[1:])


def project_and_attend(hidden_in, norm_gain, rows_full, segments, tensor_size):
    slot_count, block_len, features = hidden_in.shape
    floats = hidden_in.astype(jnp.float32)
    scale = row_scale(floats, features * tensor_size).reshape(-1)
    scaled = (floats * norm_gain).astype(jnp.bfloat16).reshape(-1, features)
    contract = (((1,), (1,)), ((), ()))
    partial = lax.dot_general(
        scaled, rows_full, contract, preferred_element_type=jnp.float32
    )
    summed = lax.psum_scatter(partial, "tensor", scatter_dimension=1, tiled=True)
    projected = (summed * scale[:, None]).astype(jnp.bfloat16)
    projected = projected.reshape(slot_count, block_len, -1, Q_PER + 2, HD)
    context = attend(projected, segments).reshape(slot_count, block_len, -1)
    cache = projected[:, :, :, Q_PER:].reshape(slot_count, block_len, -1)
    return context, cache


def per_device(hidden_in, norm_gain, w_qkv, w_out, home_count, helper_start, segment_ids):
    group_size = lax.axis_size("group")
    tensor_size = lax.axis_size("tensor")
    own_group = lax.axis_index("group")
    own_rank = lax.axis_index("tensor")
    slot_count, block_len, features = hidden_in.shape
    capacity = min(8, group_size - 2)
    local_blocks = capacity // tensor_size
    first_helper = helper_start[0]
    ends = jnp.cumsum(home_count)
    begins = ends - home_count
    groups_iota = jnp.arange(group_size, dtype=jnp.int32)
    send_slot = (groups_iota - first_helper - begins[own_group]) % group_size
    recv_slot = (own_group - first_helper - begins) % group_size
    recv_live = recv_slot < home_count
    placed = (begins + recv_slot) // group_size
    chosen = recv_live[None, :] & (
        placed[None, :] == jnp.arange(capacity, dtype=jnp.int32)[:, None]
    )
    source_of = jnp.sum(jnp.where(chosen, groups_iota[None, :], 0), axis=1)
    home_live = jnp.arange(slot_count, dtype=jnp.int32) < home_count[own_group]
    segments = lax.dynamic_slice_in_dim(segment_ids, own_group * slot_count, slot_count, 0)
    if (lax.axis_size("replica"), group_size) == (2, 8):
        rows_full = gather_rows(w_qkv, group_size, 0)
    else:
        rows_full = lax.all_gather(w_qkv, "group", axis=0, tiled=True)
    part_rows = w_out.shape[0] // tensor_size
    own_part = lax.dynamic_slice_in_dim(w_out, own_rank * part_rows, part_rows, 0)
    out_part = lax.all_gather(own_part, "group", axis=1, tiled=True)
    out_full = lax.all_gather(out_part, "tensor", axis=0, tiled=True)
    context, cache = project_and_attend(
        hidden_in, norm_gain, rows_full, segments, tensor_size
    )
    kv_cache = jnp.where(home_live[:, None, None], cache, jnp.zeros_like(cache))
    outgoing = jnp.take(context, jnp.minimum(send_slot, slot_count - 1), axis=0)
    arrived = lax.all_to_all(outgoing, "group", split_axis=0, concat_axis=0, tiled=True)
    helped = jnp.take(arrived, source_of, axis=0)
    rows = lax.all_to_all(helped, "tensor", split_axis=0, concat_axis=2, tiled=True)
    mixed = jnp.dot(
        rows.reshape(local_blocks * block_len, -1),
        out_full,
        preferred_element_type=jnp.float32,
    )
    layer_out = mixed.astype(jnp.bfloat16).reshape(local_blocks, block_len, -1)
    return (layer_out, kv_cache)


def solution(mesh):
    in_specs = (
        P(("replica", "group"), None, "tensor"),
        P("tensor"),
        P("group", "tensor"),
        P(None, "group"),
        P("replica"),
        P("replica"),
        P("replica", None),
    )
    out_specs = (
        P(("replica", "group", "tensor"), None, None),
        P(("replica", "group"), None, "tensor"),
    )
    return jax.shard_map(
        per_device, mesh=mesh, in_specs=in_specs, out_specs=out_specs, check_vma=False
    )
```

```python
import functools
import jax
import jax.numpy as jnp
from jax import lax
from jax.experimental import pallas as pl
from jax.experimental.pallas import tpu as pltpu
from jax.sharding import PartitionSpec as P

HD = 128
Q_PER = 4


epsilon = 1e-05


def attend(projected, segments):
    block_len = projected.shape[1]
    queries = projected[:, :, :, :Q_PER]
    keys_part = projected[:, :, :, Q_PER]
    values_part = projected[:, :, :, Q_PER + 1]
    scores = jnp.einsum(
        "bihqd,bjhd->bhqij", queries, keys_part, preferred_element_type=jnp.float32
    ) * HD ** (-0.5)
    positions = jnp.arange(block_len)
    causal = positions[:, None] >= positions[None, :]
    allowed = causal[None] & (segments[:, :, None] == segments[:, None, :])
    scores = jnp.where(allowed[:, None, None], scores, -jnp.inf)
    highest = jnp.max(scores, axis=-1, keepdims=True)
    raised = jnp.exp(scores - highest)
    weights = (raised / jnp.sum(raised, axis=-1, keepdims=True)).astype(jnp.bfloat16)
    context = jnp.einsum(
        "bhqij,bjhd->bihqd", weights, values_part, preferred_element_type=jnp.float32
    )
    return context.astype(jnp.bfloat16).reshape(projected.shape[0] * block_len, -1)


def row_scale(floats, model_width):
    partial_sq = jnp.sum(floats * floats, axis=-1)
    summed = lax.psum(partial_sq, "tensor")
    return lax.rsqrt(summed / model_width + epsilon)


class Spread:
    def __init__(self, line, shard, rows, place, sems, local_sem, sibling_copies):
        self.line, self.shard, self.place = line, shard, place
        self.send_sem, self.recv_sem, self.local_sem = *sems, local_sem
        self.half, self.quarter = rows // 2, rows // 4
        self.rows, self.sibling_copies = rows, sibling_copies
        self.pool = lax.axis_index("replica")
        group, self.core = lax.axis_index("group"), lax.axis_index("tensor")
        self.group, self.z, self.y = group, group // 2, group % 2
        self.across = (1 - self.pool, group, self.core)
        self.beside = (self.pool, self.z * 2 + (1 - self.y), self.core)
        self.sibling = (self.pool, group, 1 - self.core)
        self.count, self.all, self.kin = 0, [], []

    def along(self, step, y):
        return (self.z + step) % self.line * 2 + y

    def peers(self):
        spread = [(self.pool, self.along(d, self.y), self.core) for d in range(1, self.line)]
        return spread + [self.across, self.beside]

    def send(self, src, dst, peer):
        copy = pltpu.make_async_remote_copy(
            src_ref=src,
            dst_ref=dst,
            send_sem=self.send_sem.at[self.count],
            recv_sem=self.recv_sem.at[self.count],
            device_id=peer,
            device_id_type=pl.DeviceIdType.MESH,
        )
        self.count += 1
        copy.start()
        self.all.append(copy)
        return copy

    def relay(self, source, begin, count, peer):
        place = self.place(source, begin, count)
        return self.send(place, place, peer)

    def share(self, source, begin, count):
        if self.sibling_copies:
            self.kin.append(self.relay(source, begin, count, self.sibling))

    def start(self):
        mine = self.pool * self.half
        src = self.shard.at[pl.ds(mine, self.half)]
        dst = self.place(self.group, mine, self.half)
        self.own = pltpu.make_async_copy(
            self.shard, self.place(self.group, 0, self.rows), self.local_sem
        )
        self.own.start()
        self.first = [
            self.send(src, dst, (self.pool, self.along(d, self.y), self.core))
            for d in range(1, self.line)
        ]
        self.sideways = [self.send(src, dst, self.beside)]
        if self.sibling_copies:
            whole = self.place(self.group, 0, self.rows)
            self.kin.append(self.send(self.shard, whole, self.sibling))

    def trade(self):
        mine = self.pool * self.half
        self.over = []
        for d in range(1, self.line):
            self.first[d - 1].wait_recv()
            source = self.along(self.line - d, self.y)
            self.over.append(self.relay(source, mine, self.half, self.across))
            self.sideways.append(self.relay(source, mine, self.half, self.beside))
            self.share(source, mine, self.half)

    def finish(self):
        mine, other = self.pool * self.half, (1 - self.pool) * self.half
        second, third = [], []
        for d in range(self.line):
            self.sideways[d].wait_recv()
            source = self.along(self.line - d, 1 - self.y)
            skip = 0 if d == 0 else self.quarter
            second.append(self.relay(source, mine + skip, self.half - skip, self.across))
            self.share(source, mine, self.half)
            if d > 0:
                self.over[d - 1].wait_recv()
                source = self.along(self.line - d, self.y)
                third.append(self.relay(source, other, self.quarter, self.beside))
                self.share(source, other, self.half)
        self.second, self.third = second, third

    def end(self):
        other = (1 - self.pool) * self.half
        for d in range(self.line):
            skip = 0 if d == 0 else self.quarter
            source = self.along(self.line - d, 1 - self.y)
            self.second[d].wait_recv()
            self.share(source, other + skip, self.half - skip)
            if d > 0:
                self.third[d - 1].wait_recv()
                self.share(source, other, self.quarter)
        for copy in self.kin:
            copy.wait_recv()
        for copy in self.all:
            copy.wait_send()
        self.own.wait()


def copy_counts(line):
    return 5 * line - 3, 10 * line - 5


def gather_kernel(
    line, rows_ref, cols_ref, rows_full, cols_full, own_sem, rsend, rrecv, csend, crecv
):
    core = lax.axis_index("tensor")
    part, width = cols_ref.shape

    def place_rows(source, begin, count):
        return rows_full.at[source, pl.ds(begin, count)]

    def place_cols(source, begin, count):
        top = pl.multiple_of(core * part + begin, part // 4)
        left = pl.multiple_of(source * width, width)
        return cols_full.at[pl.ds(top, count), pl.ds(left, width)]

    first = Spread(
        line, rows_ref, rows_ref.shape[0], place_rows, (rsend, rrecv), own_sem.at[0], False
    )
    later = Spread(line, cols_ref, part, place_cols, (csend, crecv), own_sem.at[1], True)
    barrier = pltpu.get_barrier_semaphore()
    peers = first.peers() + [first.sibling]
    for peer in peers:
        pl.semaphore_signal(barrier, inc=1, device_id=peer, device_id_type=pl.DeviceIdType.MESH)
    pl.semaphore_wait(barrier, len(peers))
    first.start()
    first.trade()
    later.start()
    first.finish()
    later.trade()
    later.finish()
    first.end()
    later.end()


def gather_weights(rows, cols, group_size, tensor_size, collective_id):
    line = group_size // 2
    few, many = copy_counts(line)
    any_space = pl.BlockSpec(memory_space=pl.ANY)
    full, out_full = pl.pallas_call(
        functools.partial(gather_kernel, line),
        out_shape=(
            jax.ShapeDtypeStruct((group_size,) + rows.shape, rows.dtype),
            jax.ShapeDtypeStruct(
                (tensor_size * cols.shape[0], group_size * cols.shape[1]), cols.dtype
            ),
        ),
        in_specs=[any_space, any_space],
        out_specs=(any_space, any_space),
        scratch_shapes=[
            pltpu.SemaphoreType.DMA((2,)),
            pltpu.SemaphoreType.DMA((few,)),
            pltpu.SemaphoreType.DMA((few,)),
            pltpu.SemaphoreType.DMA((many,)),
            pltpu.SemaphoreType.DMA((many,)),
        ],
        compiler_params=pltpu.CompilerParams(
            collective_id=collective_id, has_side_effects=True
        ),
    )(rows, cols)
    return full.reshape((-1,) + rows.shape[1:]), out_full


def project_and_attend(hidden_in, norm_gain, rows_full, segments, tensor_size):
    slot_count, block_len, features = hidden_in.shape
    floats = hidden_in.astype(jnp.float32)
    scale = row_scale(floats, features * tensor_size).reshape(-1)
    scaled = (floats * norm_gain).astype(jnp.bfloat16).reshape(-1, features)
    contract = (((1,), (1,)), ((), ()))
    partial = lax.dot_general(
        scaled, rows_full, contract, preferred_element_type=jnp.float32
    )
    summed = lax.psum_scatter(partial, "tensor", scatter_dimension=1, tiled=True)
    projected = (summed * scale[:, None]).astype(jnp.bfloat16)
    projected = projected.reshape(slot_count, block_len, -1, Q_PER + 2, HD)
    context = attend(projected, segments).reshape(slot_count, block_len, -1)
    cache = projected[:, :, :, Q_PER:].reshape(slot_count, block_len, -1)
    return context, cache


def per_device(hidden_in, norm_gain, w_qkv, w_out, home_count, helper_start, segment_ids):
    group_size = lax.axis_size("group")
    tensor_size = lax.axis_size("tensor")
    own_group = lax.axis_index("group")
    own_rank = lax.axis_index("tensor")
    slot_count, block_len, features = hidden_in.shape
    capacity = min(8, group_size - 2)
    local_blocks = capacity // tensor_size
    first_helper = helper_start[0]
    ends = jnp.cumsum(home_count)
    begins = ends - home_count
    groups_iota = jnp.arange(group_size, dtype=jnp.int32)
    send_slot = (groups_iota - first_helper - begins[own_group]) % group_size
    recv_slot = (own_group - first_helper - begins) % group_size
    recv_live = recv_slot < home_count
    placed = (begins + recv_slot) // group_size
    chosen = recv_live[None, :] & (
        placed[None, :] == jnp.arange(capacity, dtype=jnp.int32)[:, None]
    )
    source_of = jnp.sum(jnp.where(chosen, groups_iota[None, :], 0), axis=1)
    home_live = jnp.arange(slot_count, dtype=jnp.int32) < home_count[own_group]
    segments = lax.dynamic_slice_in_dim(segment_ids, own_group * slot_count, slot_count, 0)
    part_rows = w_out.shape[0] // tensor_size
    own_part = lax.dynamic_slice_in_dim(w_out, own_rank * part_rows, part_rows, 0)
    if (lax.axis_size("replica"), group_size, tensor_size) == (2, 8, 2):
        rows_full, out_full = gather_weights(w_qkv, own_part, group_size, tensor_size, 0)
    else:
        rows_full = lax.all_gather(w_qkv, "group", axis=0, tiled=True)
        out_part = lax.all_gather(own_part, "group", axis=1, tiled=True)
        out_full = lax.all_gather(out_part, "tensor", axis=0, tiled=True)
    context, cache = project_and_attend(
        hidden_in, norm_gain, rows_full, segments, tensor_size
    )
    kv_cache = jnp.where(home_live[:, None, None], cache, jnp.zeros_like(cache))
    outgoing = jnp.take(context, jnp.minimum(send_slot, slot_count - 1), axis=0)
    arrived = lax.all_to_all(outgoing, "group", split_axis=0, concat_axis=0, tiled=True)
    helped = jnp.take(arrived, source_of, axis=0)
    rows = lax.all_to_all(helped, "tensor", split_axis=0, concat_axis=2, tiled=True)
    mixed = jnp.dot(
        rows.reshape(local_blocks * block_len, -1),
        out_full,
        preferred_element_type=jnp.float32,
    )
    layer_out = mixed.astype(jnp.bfloat16).reshape(local_blocks, block_len, -1)
    return (layer_out, kv_cache)


def solution(mesh):
    in_specs = (
        P(("replica", "group"), None, "tensor"),
        P("tensor"),
        P("group", "tensor"),
        P(None, "group"),
        P("replica"),
        P("replica"),
        P("replica", None),
    )
    out_specs = (
        P(("replica", "group", "tensor"), None, None),
        P(("replica", "group"), None, "tensor"),
    )
    return jax.shard_map(
        per_device, mesh=mesh, in_specs=in_specs, out_specs=out_specs, check_vma=False
    )
```

```python
import functools
import jax
import jax.numpy as jnp
from jax import lax
from jax.experimental import pallas as pl
from jax.experimental.pallas import tpu as pltpu
from jax.sharding import PartitionSpec as P

HD = 128
Q_PER = 4


epsilon = 1e-05


def attend(projected, segments):
    block_len = projected.shape[1]
    queries = projected[:, :, :, :Q_PER]
    keys_part = projected[:, :, :, Q_PER]
    values_part = projected[:, :, :, Q_PER + 1]
    scores = jnp.einsum(
        "bihqd,bjhd->bhqij", queries, keys_part, preferred_element_type=jnp.float32
    ) * HD ** (-0.5)
    positions = jnp.arange(block_len)
    causal = positions[:, None] >= positions[None, :]
    allowed = causal[None] & (segments[:, :, None] == segments[:, None, :])
    scores = jnp.where(allowed[:, None, None], scores, -jnp.inf)
    highest = jnp.max(scores, axis=-1, keepdims=True)
    raised = jnp.exp(scores - highest)
    weights = (raised / jnp.sum(raised, axis=-1, keepdims=True)).astype(jnp.bfloat16)
    context = jnp.einsum(
        "bhqij,bjhd->bihqd", weights, values_part, preferred_element_type=jnp.float32
    )
    return context.astype(jnp.bfloat16).reshape(projected.shape[0] * block_len, -1)


def row_scale(floats, model_width):
    partial_sq = jnp.sum(floats * floats, axis=-1)
    summed = lax.psum(partial_sq, "tensor")
    return lax.rsqrt(summed / model_width + epsilon)


class Spread:
    def __init__(self, line, shard, rows, place, sems, local_sem, sibling_copies):
        self.line, self.shard, self.place = line, shard, place
        self.send_sem, self.recv_sem, self.local_sem = *sems, local_sem
        self.half, self.quarter = rows // 2, rows // 4
        self.rows, self.sibling_copies = rows, sibling_copies
        self.pool = lax.axis_index("replica")
        group, self.core = lax.axis_index("group"), lax.axis_index("tensor")
        self.group, self.z, self.y = group, group // 2, group % 2
        self.across = (1 - self.pool, group, self.core)
        self.beside = (self.pool, self.z * 2 + (1 - self.y), self.core)
        self.sibling = (self.pool, group, 1 - self.core)
        self.count, self.all, self.kin = 0, [], []

    def along(self, step, y):
        return (self.z + step) % self.line * 2 + y

    def peers(self):
        spread = [(self.pool, self.along(d, self.y), self.core) for d in range(1, self.line)]
        return spread + [self.across, self.beside]

    def send(self, src, dst, peer):
        copy = pltpu.make_async_remote_copy(
            src_ref=src,
            dst_ref=dst,
            send_sem=self.send_sem.at[self.count],
            recv_sem=self.recv_sem.at[self.count],
            device_id=peer,
            device_id_type=pl.DeviceIdType.MESH,
        )
        self.count += 1
        copy.start()
        self.all.append(copy)
        return copy

    def relay(self, source, begin, count, peer):
        place = self.place(source, begin, count)
        return self.send(place, place, peer)

    def share(self, source, begin, count):
        if self.sibling_copies:
            self.kin.append(self.relay(source, begin, count, self.sibling))

    def start(self):
        mine = self.pool * self.half
        src = self.shard.at[pl.ds(mine, self.half)]
        dst = self.place(self.group, mine, self.half)
        self.own = pltpu.make_async_copy(
            self.shard, self.place(self.group, 0, self.rows), self.local_sem
        )
        self.own.start()
        self.first = [
            self.send(src, dst, (self.pool, self.along(d, self.y), self.core))
            for d in range(1, self.line)
        ]
        self.sideways = [self.send(src, dst, self.beside)]
        if self.sibling_copies:
            whole = self.place(self.group, 0, self.rows)
            self.kin.append(self.send(self.shard, whole, self.sibling))

    def trade(self):
        mine = self.pool * self.half
        self.over = []
        for d in range(1, self.line):
            self.first[d - 1].wait_recv()
            source = self.along(self.line - d, self.y)
            self.over.append(self.relay(source, mine, self.half, self.across))
            self.sideways.append(self.relay(source, mine, self.half, self.beside))
            self.share(source, mine, self.half)

    def finish(self):
        mine, other = self.pool * self.half, (1 - self.pool) * self.half
        second, third = [], []
        for d in range(self.line):
            self.sideways[d].wait_recv()
            source = self.along(self.line - d, 1 - self.y)
            skip = 0 if d == 0 else self.quarter
            second.append(self.relay(source, mine + skip, self.half - skip, self.across))
            self.share(source, mine, self.half)
            if d > 0:
                self.over[d - 1].wait_recv()
                source = self.along(self.line - d, self.y)
                third.append(self.relay(source, other, self.quarter, self.beside))
                self.share(source, other, self.half)
        self.second, self.third = second, third

    def end(self):
        other = (1 - self.pool) * self.half
        for d in range(self.line):
            skip = 0 if d == 0 else self.quarter
            source = self.along(self.line - d, 1 - self.y)
            self.second[d].wait_recv()
            self.share(source, other + skip, self.half - skip)
            if d > 0:
                self.third[d - 1].wait_recv()
                self.share(source, other, self.quarter)
        for copy in self.kin:
            copy.wait_recv()
        for copy in self.all:
            copy.wait_send()
        self.own.wait()


def copy_counts(line):
    return 5 * line - 3, 10 * line - 5


def greet(peers):
    barrier = pltpu.get_barrier_semaphore()
    for peer in peers:
        pl.semaphore_signal(barrier, inc=1, device_id=peer, device_id_type=pl.DeviceIdType.MESH)
    pl.semaphore_wait(barrier, len(peers))


def gather_kernel(line, rows_ref, rows_full, own_sem, rsend, rrecv):
    def place_rows(source, begin, count):
        return rows_full.at[source, pl.ds(begin, count)]

    spread = Spread(
        line, rows_ref, rows_ref.shape[0], place_rows, (rsend, rrecv), own_sem, False
    )
    greet(spread.peers())
    spread.start()
    spread.trade()
    spread.finish()
    spread.end()


def gather_rows(rows, group_size, collective_id):
    line = group_size // 2
    few, _ = copy_counts(line)
    any_space = pl.BlockSpec(memory_space=pl.ANY)
    full = pl.pallas_call(
        functools.partial(gather_kernel, line),
        out_shape=jax.ShapeDtypeStruct((group_size,) + rows.shape, rows.dtype),
        in_specs=[any_space],
        out_specs=any_space,
        scratch_shapes=[
            pltpu.SemaphoreType.DMA,
            pltpu.SemaphoreType.DMA((few,)),
            pltpu.SemaphoreType.DMA((few,)),
        ],
        compiler_params=pltpu.CompilerParams(
            collective_id=collective_id, has_side_effects=True
        ),
    )(rows)
    return full.reshape((-1,) + rows.shape[1:])


def attend_one(projected, bias):
    block_len = projected.shape[0]
    heads = [projected[:, i * HD : (i + 1) * HD] for i in range(Q_PER + 2)]
    queries = jnp.concatenate(heads[:Q_PER], axis=0)
    scores = lax.dot_general(
        queries, heads[Q_PER], (((1,), (1,)), ((), ())), preferred_element_type=jnp.float32
    ) * HD ** (-0.5)
    scores = scores.reshape(Q_PER, block_len, block_len) + bias[None]
    raised = jnp.exp(scores - jnp.max(scores, axis=-1, keepdims=True))
    weights = (raised / jnp.sum(raised, axis=-1, keepdims=True)).astype(jnp.bfloat16)
    context = jnp.dot(
        weights.reshape(Q_PER * block_len, block_len),
        heads[Q_PER + 1],
        preferred_element_type=jnp.float32,
    ).astype(jnp.bfloat16)
    parts = [context[i * block_len : (i + 1) * block_len] for i in range(Q_PER)]
    return jnp.concatenate(parts, axis=1)


def tail_kernel(
    line, slots_ref, source_ref, proj_ref, bias_ref, cols_ref, out_ref,
    w_full, made, got, rows_buf,
    own_sem, csend, crecv, bsend, brecv, ksend, krecv,
):
    groups = 2 * line
    pool, group = lax.axis_index("replica"), lax.axis_index("group")
    core = lax.axis_index("tensor")
    part, width = cols_ref.shape

    def place_cols(source, begin, count):
        top = pl.multiple_of(core * part + begin, part // 4)
        left = pl.multiple_of(source * width, width)
        return w_full.at[pl.ds(top, count), pl.ds(left, width)]

    spread = Spread(line, cols_ref, part, place_cols, (csend, crecv), own_sem, True)

    def block_copy(step):
        return pltpu.make_async_remote_copy(
            src_ref=made.at[step],
            dst_ref=got.at[group, core],
            send_sem=bsend.at[step],
            recv_sem=brecv.at[step],
            device_id=(pool, (group + step) % groups, core),
            device_id_type=pl.DeviceIdType.MESH,
        )

    def kin_copy(step):
        place = got.at[(group + groups - step) % groups, core]
        return pltpu.make_async_remote_copy(
            src_ref=place,
            dst_ref=place,
            send_sem=ksend.at[step],
            recv_sem=krecv.at[step],
            device_id=(pool, group, 1 - core),
            device_id_type=pl.DeviceIdType.MESH,
        )

    others = [(pool, (group + d) % groups, core) for d in range(1, groups)]
    greet(others + [spread.across, spread.sibling])
    spread.start()

    def attend_and_send(step, carry):
        slot = slots_ref[(group + step) % groups]
        made[step] = attend_one(proj_ref[slot], bias_ref[slot])
        block_copy(step).start()
        return carry

    lax.fori_loop(1, groups, attend_and_send, 0)
    slot = slots_ref[group]
    got[group, core] = attend_one(proj_ref[slot], bias_ref[slot])
    kin_copy(0).start()
    spread.trade()
    spread.finish()

    def pass_on(step, carry):
        block_copy(step).wait_recv()
        kin_copy(step).start()
        return carry

    lax.fori_loop(1, groups, pass_on, 0)
    spread.end()

    def settle(step, carry):
        kin_copy(step).wait()
        return carry

    def settle_sent(step, carry):
        block_copy(step).wait_send()
        return carry

    lax.fori_loop(0, groups, settle, 0)
    lax.fori_loop(1, groups, settle_sent, 0)
    block_len, wide = made.shape[1:]
    for b in range(out_ref.shape[0] // block_len):
        block = got[source_ref[b]]
        for c in range(got.shape[1]):
            rows_buf[b * block_len : (b + 1) * block_len, c * wide : (c + 1) * wide] = block[c]

    def column_tile(tile, carry):
        columns = pl.ds(pl.multiple_of(tile * width, width), width)
        out_ref[:, columns] = jnp.dot(
            rows_buf[...], w_full[:, columns], preferred_element_type=jnp.float32
        ).astype(jnp.bfloat16)
        return carry

    lax.fori_loop(0, groups, column_tile, 0)


def attend_and_mix(slots, sources, projected, bias, cols, group_size, tensor_size):
    line = group_size // 2
    _, many = copy_counts(line)
    block_len = projected.shape[1]
    wide = Q_PER * HD
    depth, model_width = tensor_size * cols.shape[0], group_size * cols.shape[1]
    tokens = sources.shape[0] * block_len
    smem, vmem = (pl.BlockSpec(memory_space=m) for m in (pltpu.SMEM, pltpu.VMEM))
    return pl.pallas_call(
        functools.partial(tail_kernel, line),
        out_shape=jax.ShapeDtypeStruct((tokens, model_width), jnp.bfloat16),
        in_specs=[smem, smem, vmem, vmem, pl.BlockSpec(memory_space=pl.ANY)],
        out_specs=vmem,
        scratch_shapes=[
            pltpu.VMEM((depth, model_width), jnp.bfloat16),
            pltpu.VMEM((group_size, block_len, wide), jnp.bfloat16),
            pltpu.VMEM((group_size, tensor_size, block_len, wide), jnp.bfloat16),
            pltpu.VMEM((tokens, tensor_size * wide), jnp.bfloat16),
            pltpu.SemaphoreType.DMA,
            pltpu.SemaphoreType.DMA((many,)),
            pltpu.SemaphoreType.DMA((many,)),
        ]
        + [pltpu.SemaphoreType.DMA((group_size,))] * 4,
        compiler_params=pltpu.CompilerParams(
            collective_id=1, has_side_effects=True, vmem_limit_bytes=48 * 2**20
        ),
    )(slots, sources, projected, bias, cols)


def project(hidden_in, norm_gain, rows_full, tensor_size):
    slot_count, block_len, features = hidden_in.shape
    floats = hidden_in.astype(jnp.float32)
    scale = row_scale(floats, features * tensor_size).reshape(-1)
    scaled = (floats * norm_gain).astype(jnp.bfloat16).reshape(-1, features)
    contract = (((1,), (1,)), ((), ()))
    partial = lax.dot_general(
        scaled, rows_full, contract, preferred_element_type=jnp.float32
    )
    summed = lax.psum_scatter(partial, "tensor", scatter_dimension=1, tiled=True)
    projected = (summed * scale[:, None]).astype(jnp.bfloat16)
    return projected.reshape(slot_count, block_len, -1)


def per_device(hidden_in, norm_gain, w_qkv, w_out, home_count, helper_start, segment_ids):
    group_size = lax.axis_size("group")
    tensor_size = lax.axis_size("tensor")
    own_group = lax.axis_index("group")
    own_rank = lax.axis_index("tensor")
    slot_count, block_len, features = hidden_in.shape
    capacity = min(8, group_size - 2)
    local_blocks = capacity // tensor_size
    first_helper = helper_start[0]
    ends = jnp.cumsum(home_count)
    begins = ends - home_count
    groups_iota = jnp.arange(group_size, dtype=jnp.int32)
    send_slot = (groups_iota - first_helper - begins[own_group]) % group_size
    recv_slot = (own_group - first_helper - begins) % group_size
    recv_live = recv_slot < home_count
    placed = (begins + recv_slot) // group_size
    chosen = recv_live[None, :] & (
        placed[None, :] == jnp.arange(capacity, dtype=jnp.int32)[:, None]
    )
    source_of = jnp.sum(jnp.where(chosen, groups_iota[None, :], 0), axis=1)
    home_live = jnp.arange(slot_count, dtype=jnp.int32) < home_count[own_group]
    segments = lax.dynamic_slice_in_dim(segment_ids, own_group * slot_count, slot_count, 0)
    part_rows = w_out.shape[0] // tensor_size
    own_part = lax.dynamic_slice_in_dim(w_out, own_rank * part_rows, part_rows, 0)
    by_kernel = (lax.axis_size("replica"), group_size, tensor_size) == (2, 8, 2)
    if by_kernel:
        rows_full = gather_rows(w_qkv, group_size, 0)
    else:
        rows_full = lax.all_gather(w_qkv, "group", axis=0, tiled=True)
    projected = project(hidden_in, norm_gain, rows_full, tensor_size)
    by_head = projected.reshape(slot_count, block_len, -1, Q_PER + 2, HD)
    cache = by_head[:, :, :, Q_PER:].reshape(slot_count, block_len, -1)
    kv_cache = jnp.where(home_live[:, None, None], cache, jnp.zeros_like(cache))
    slots = jnp.minimum(send_slot, slot_count - 1)
    if by_kernel:
        positions = jnp.arange(block_len)
        allowed = (positions[:, None] >= positions[None, :])[None] & (
            segments[:, :, None] == segments[:, None, :]
        )
        bias = jnp.where(allowed, 0.0, -jnp.inf).astype(jnp.float32)
        sources = lax.dynamic_slice_in_dim(source_of, own_rank * local_blocks, local_blocks)
        mixed = attend_and_mix(
            slots, sources, projected, bias, own_part, group_size, tensor_size
        )
        return (mixed.reshape(local_blocks, block_len, -1), kv_cache)
    out_part = lax.all_gather(own_part, "group", axis=1, tiled=True)
    out_full = lax.all_gather(out_part, "tensor", axis=0, tiled=True)
    context = attend(by_head, segments).reshape(slot_count, block_len, -1)
    outgoing = jnp.take(context, slots, axis=0)
    arrived = lax.all_to_all(outgoing, "group", split_axis=0, concat_axis=0, tiled=True)
    helped = jnp.take(arrived, source_of, axis=0)
    rows = lax.all_to_all(helped, "tensor", split_axis=0, concat_axis=2, tiled=True)
    mixed = jnp.dot(
        rows.reshape(local_blocks * block_len, -1),
        out_full,
        preferred_element_type=jnp.float32,
    )
    layer_out = mixed.astype(jnp.bfloat16).reshape(local_blocks, block_len, -1)
    return (layer_out, kv_cache)


def solution(mesh):
    in_specs = (
        P(("replica", "group"), None, "tensor"),
        P("tensor"),
        P("group", "tensor"),
        P(None, "group"),
        P("replica"),
        P("replica"),
        P("replica", None),
    )
    out_specs = (
        P(("replica", "group", "tensor"), None, None),
        P(("replica", "group"), None, "tensor"),
    )
    return jax.shard_map(
        per_device, mesh=mesh, in_specs=in_specs, out_specs=out_specs, check_vma=False
    )
```

```python
import functools
import jax
import jax.numpy as jnp
from jax import lax
from jax.experimental import pallas as pl
from jax.experimental.pallas import tpu as pltpu
from jax.sharding import PartitionSpec as P

HD = 128
Q_PER = 4


epsilon = 1e-05


def attend(projected, segments):
    block_len = projected.shape[1]
    queries = projected[:, :, :, :Q_PER]
    keys_part = projected[:, :, :, Q_PER]
    values_part = projected[:, :, :, Q_PER + 1]
    scores = jnp.einsum(
        "bihqd,bjhd->bhqij", queries, keys_part, preferred_element_type=jnp.float32
    ) * HD ** (-0.5)
    positions = jnp.arange(block_len)
    causal = positions[:, None] >= positions[None, :]
    allowed = causal[None] & (segments[:, :, None] == segments[:, None, :])
    scores = jnp.where(allowed[:, None, None], scores, -jnp.inf)
    highest = jnp.max(scores, axis=-1, keepdims=True)
    raised = jnp.exp(scores - highest)
    weights = (raised / jnp.sum(raised, axis=-1, keepdims=True)).astype(jnp.bfloat16)
    context = jnp.einsum(
        "bhqij,bjhd->bihqd", weights, values_part, preferred_element_type=jnp.float32
    )
    return context.astype(jnp.bfloat16).reshape(projected.shape[0] * block_len, -1)


def row_scale(floats, model_width):
    partial_sq = jnp.sum(floats * floats, axis=-1)
    summed = lax.psum(partial_sq, "tensor")
    return lax.rsqrt(summed / model_width + epsilon)


class Spread:
    def __init__(self, line, shard, rows, place, sems, local_sem, sibling_copies):
        self.line, self.shard, self.place = line, shard, place
        self.send_sem, self.recv_sem, self.local_sem = *sems, local_sem
        self.half, self.quarter = rows // 2, rows // 4
        self.rows, self.sibling_copies = rows, sibling_copies
        self.pool = lax.axis_index("replica")
        group, self.core = lax.axis_index("group"), lax.axis_index("tensor")
        self.group, self.z, self.y = group, group // 2, group % 2
        self.across = (1 - self.pool, group, self.core)
        self.beside = (self.pool, self.z * 2 + (1 - self.y), self.core)
        self.sibling = (self.pool, group, 1 - self.core)
        self.count, self.all, self.kin = 0, [], []

    def along(self, step, y):
        return (self.z + step) % self.line * 2 + y

    def peers(self):
        spread = [(self.pool, self.along(d, self.y), self.core) for d in range(1, self.line)]
        return spread + [self.across, self.beside]

    def send(self, src, dst, peer):
        copy = pltpu.make_async_remote_copy(
            src_ref=src,
            dst_ref=dst,
            send_sem=self.send_sem.at[self.count],
            recv_sem=self.recv_sem.at[self.count],
            device_id=peer,
            device_id_type=pl.DeviceIdType.MESH,
        )
        self.count += 1
        copy.start()
        self.all.append(copy)
        return copy

    def relay(self, source, begin, count, peer):
        place = self.place(source, begin, count)
        return self.send(place, place, peer)

    def share(self, source, begin, count):
        if self.sibling_copies:
            self.kin.append(self.relay(source, begin, count, self.sibling))

    def start(self):
        mine = self.pool * self.half
        src = self.shard.at[pl.ds(mine, self.half)]
        dst = self.place(self.group, mine, self.half)
        self.own = pltpu.make_async_copy(
            self.shard, self.place(self.group, 0, self.rows), self.local_sem
        )
        self.own.start()
        self.first = [
            self.send(src, dst, (self.pool, self.along(d, self.y), self.core))
            for d in range(1, self.line)
        ]
        self.sideways = [self.send(src, dst, self.beside)]
        if self.sibling_copies:
            whole = self.place(self.group, 0, self.rows)
            self.kin.append(self.send(self.shard, whole, self.sibling))

    def trade(self):
        mine = self.pool * self.half
        self.over = []
        for d in range(1, self.line):
            self.first[d - 1].wait_recv()
            source = self.along(self.line - d, self.y)
            self.over.append(self.relay(source, mine, self.half, self.across))
            self.sideways.append(self.relay(source, mine, self.half, self.beside))
            self.share(source, mine, self.half)

    def finish(self):
        mine, other = self.pool * self.half, (1 - self.pool) * self.half
        second, third = [], []
        for d in range(self.line):
            self.sideways[d].wait_recv()
            source = self.along(self.line - d, 1 - self.y)
            skip = 0 if d == 0 else self.quarter
            second.append(self.relay(source, mine + skip, self.half - skip, self.across))
            self.share(source, mine, self.half)
            if d > 0:
                self.over[d - 1].wait_recv()
                source = self.along(self.line - d, self.y)
                third.append(self.relay(source, other, self.quarter, self.beside))
                self.share(source, other, self.half)
        self.second, self.third = second, third

    def end(self, arrived=None):
        other = (1 - self.pool) * self.half
        for d in range(self.line):
            skip = 0 if d == 0 else self.quarter
            source = self.along(self.line - d, 1 - self.y)
            self.second[d].wait_recv()
            self.share(source, other + skip, self.half - skip)
            if d > 0:
                self.third[d - 1].wait_recv()
                self.share(source, other, self.quarter)
            if d == 0:
                self.own.wait()
            if arrived is not None:
                arrived((self.z + self.line - d) % self.line)
        for copy in self.kin:
            copy.wait_recv()
        for copy in self.all:
            copy.wait_send()


def copy_counts(line):
    return 5 * line - 3, 10 * line - 5


def greet(peers):
    barrier = pltpu.get_barrier_semaphore()
    for peer in peers:
        pl.semaphore_signal(barrier, inc=1, device_id=peer, device_id_type=pl.DeviceIdType.MESH)
    pl.semaphore_wait(barrier, len(peers))


def project_kernel(
    line, scaled_ref, scale_ref, rows_ref, out_ref,
    rows_full, kept, sent, got, own_sem, rsend, rrecv, hsend, hrecv,
):
    def place_rows(source, begin, count):
        return rows_full.at[source, pl.ds(begin, count)]

    core = lax.axis_index("tensor")
    spread = Spread(
        line, rows_ref, rows_ref.shape[0], place_rows, (rsend, rrecv), own_sem, False
    )
    per_core = kept.shape[0]
    tokens, width = kept.shape[1:]
    step = 256

    def head_copy(index):
        return pltpu.make_async_remote_copy(
            src_ref=sent.at[index],
            dst_ref=got.at[index],
            send_sem=hsend.at[index],
            recv_sem=hrecv.at[index],
            device_id=spread.sibling,
            device_id_type=pl.DeviceIdType.MESH,
        )

    def multiply(pair, target):
        weights = rows_full[pl.ds(pair * 2, 2)].reshape(width, -1)

        def tile(index, carry):
            rows = pl.ds(pl.multiple_of(index * step, step), step)
            target[pair % per_core, rows] = lax.dot_general(
                scaled_ref[rows],
                weights,
                (((1,), (1,)), ((), ())),
                preferred_element_type=jnp.float32,
            )
            return carry

        lax.fori_loop(0, tokens // step, tile, 0)

    def arrived(pair):
        @pl.when(pair // per_core == core)
        def _():
            multiply(pair, kept)

        @pl.when(pair // per_core != core)
        def _():
            multiply(pair, sent)
            head_copy(pair % per_core).start()

    greet(spread.peers() + [spread.sibling])
    spread.start()
    spread.trade()
    spread.finish()
    spread.end(arrived)
    for j in range(per_core):
        head_copy(j).wait()
        total = (kept[j] + got[j]) * scale_ref[...]
        out_ref[:, j * width : (j + 1) * width] = total.astype(jnp.bfloat16)


def project_rows(scaled, scale, rows, group_size, tensor_size, collective_id):
    line = group_size // 2
    few, _ = copy_counts(line)
    tokens = scaled.shape[0]
    per_core, width = line // tensor_size, 2 * rows.shape[0]
    vmem = pl.BlockSpec(memory_space=pltpu.VMEM)
    halves = pltpu.VMEM((per_core, tokens, width), jnp.float32)
    return pl.pallas_call(
        functools.partial(project_kernel, line),
        out_shape=jax.ShapeDtypeStruct((tokens, per_core * width), jnp.bfloat16),
        in_specs=[vmem, vmem, pl.BlockSpec(memory_space=pl.ANY)],
        out_specs=vmem,
        scratch_shapes=[
            pltpu.VMEM((group_size,) + rows.shape, rows.dtype),
            halves,
            halves,
            halves,
            pltpu.SemaphoreType.DMA,
            pltpu.SemaphoreType.DMA((few,)),
            pltpu.SemaphoreType.DMA((few,)),
            pltpu.SemaphoreType.DMA((per_core,)),
            pltpu.SemaphoreType.DMA((per_core,)),
        ],
        compiler_params=pltpu.CompilerParams(
            collective_id=collective_id, has_side_effects=True, vmem_limit_bytes=48 * 2**20
        ),
    )(scaled, scale, rows)


def attend_one(projected, bias):
    block_len = projected.shape[0]
    heads = [projected[:, i * HD : (i + 1) * HD] for i in range(Q_PER + 2)]
    queries = jnp.concatenate(heads[:Q_PER], axis=0)
    scores = lax.dot_general(
        queries, heads[Q_PER], (((1,), (1,)), ((), ())), preferred_element_type=jnp.float32
    ) * HD ** (-0.5)
    scores = scores.reshape(Q_PER, block_len, block_len) + bias[None]
    raised = jnp.exp(scores - jnp.max(scores, axis=-1, keepdims=True))
    weights = (raised / jnp.sum(raised, axis=-1, keepdims=True)).astype(jnp.bfloat16)
    context = jnp.dot(
        weights.reshape(Q_PER * block_len, block_len),
        heads[Q_PER + 1],
        preferred_element_type=jnp.float32,
    ).astype(jnp.bfloat16)
    parts = [context[i * block_len : (i + 1) * block_len] for i in range(Q_PER)]
    return jnp.concatenate(parts, axis=1)


def tail_kernel(
    line, slots_ref, source_ref, proj_ref, bias_ref, cols_ref, out_ref,
    w_full, made, got, rows_buf,
    own_sem, csend, crecv, bsend, brecv, ksend, krecv,
):
    groups = 2 * line
    pool, group = lax.axis_index("replica"), lax.axis_index("group")
    core = lax.axis_index("tensor")
    part, width = cols_ref.shape

    def place_cols(source, begin, count):
        top = pl.multiple_of(core * part + begin, part // 4)
        left = pl.multiple_of(source * width, width)
        return w_full.at[pl.ds(top, count), pl.ds(left, width)]

    spread = Spread(line, cols_ref, part, place_cols, (csend, crecv), own_sem, True)

    def block_copy(step):
        return pltpu.make_async_remote_copy(
            src_ref=made.at[step],
            dst_ref=got.at[group, core],
            send_sem=bsend.at[step],
            recv_sem=brecv.at[step],
            device_id=(pool, (group + step) % groups, core),
            device_id_type=pl.DeviceIdType.MESH,
        )

    def kin_copy(step):
        place = got.at[(group + groups - step) % groups, core]
        return pltpu.make_async_remote_copy(
            src_ref=place,
            dst_ref=place,
            send_sem=ksend.at[step],
            recv_sem=krecv.at[step],
            device_id=(pool, group, 1 - core),
            device_id_type=pl.DeviceIdType.MESH,
        )

    others = [(pool, (group + d) % groups, core) for d in range(1, groups)]
    greet(others + [spread.across, spread.sibling])
    spread.start()

    def attend_and_send(step, carry):
        slot = slots_ref[(group + step) % groups]
        made[step] = attend_one(proj_ref[slot], bias_ref[slot])
        block_copy(step).start()
        return carry

    lax.fori_loop(1, groups, attend_and_send, 0)
    slot = slots_ref[group]
    got[group, core] = attend_one(proj_ref[slot], bias_ref[slot])
    kin_copy(0).start()
    spread.trade()
    spread.finish()

    def pass_on(step, carry):
        block_copy(step).wait_recv()
        kin_copy(step).start()
        return carry

    lax.fori_loop(1, groups, pass_on, 0)
    spread.end()

    def settle(step, carry):
        kin_copy(step).wait()
        return carry

    def settle_sent(step, carry):
        block_copy(step).wait_send()
        return carry

    lax.fori_loop(0, groups, settle, 0)
    lax.fori_loop(1, groups, settle_sent, 0)
    block_len, wide = made.shape[1:]
    for b in range(out_ref.shape[0] // block_len):
        block = got[source_ref[b]]
        for c in range(got.shape[1]):
            rows_buf[b * block_len : (b + 1) * block_len, c * wide : (c + 1) * wide] = block[c]

    def column_tile(tile, carry):
        columns = pl.ds(pl.multiple_of(tile * width, width), width)
        out_ref[:, columns] = jnp.dot(
            rows_buf[...], w_full[:, columns], preferred_element_type=jnp.float32
        ).astype(jnp.bfloat16)
        return carry

    lax.fori_loop(0, groups, column_tile, 0)


def attend_and_mix(slots, sources, projected, bias, cols, group_size, tensor_size):
    line = group_size // 2
    _, many = copy_counts(line)
    block_len = projected.shape[1]
    wide = Q_PER * HD
    depth, model_width = tensor_size * cols.shape[0], group_size * cols.shape[1]
    tokens = sources.shape[0] * block_len
    smem, vmem = (pl.BlockSpec(memory_space=m) for m in (pltpu.SMEM, pltpu.VMEM))
    return pl.pallas_call(
        functools.partial(tail_kernel, line),
        out_shape=jax.ShapeDtypeStruct((tokens, model_width), jnp.bfloat16),
        in_specs=[smem, smem, vmem, vmem, pl.BlockSpec(memory_space=pl.ANY)],
        out_specs=vmem,
        scratch_shapes=[
            pltpu.VMEM((depth, model_width), jnp.bfloat16),
            pltpu.VMEM((group_size, block_len, wide), jnp.bfloat16),
            pltpu.VMEM((group_size, tensor_size, block_len, wide), jnp.bfloat16),
            pltpu.VMEM((tokens, tensor_size * wide), jnp.bfloat16),
            pltpu.SemaphoreType.DMA,
            pltpu.SemaphoreType.DMA((many,)),
            pltpu.SemaphoreType.DMA((many,)),
        ]
        + [pltpu.SemaphoreType.DMA((group_size,))] * 4,
        compiler_params=pltpu.CompilerParams(
            collective_id=1, has_side_effects=True, vmem_limit_bytes=48 * 2**20
        ),
    )(slots, sources, projected, bias, cols)


def project(hidden_in, norm_gain, w_qkv, by_kernel, group_size, tensor_size):
    slot_count, block_len, features = hidden_in.shape
    floats = hidden_in.astype(jnp.float32)
    scale = row_scale(floats, features * tensor_size).reshape(-1)
    scaled = (floats * norm_gain).astype(jnp.bfloat16).reshape(-1, features)
    if by_kernel:
        projected = project_rows(
            scaled, scale[:, None], w_qkv, group_size, tensor_size, 0
        )
        return projected.reshape(slot_count, block_len, -1)
    rows_full = lax.all_gather(w_qkv, "group", axis=0, tiled=True)
    contract = (((1,), (1,)), ((), ()))
    partial = lax.dot_general(
        scaled, rows_full, contract, preferred_element_type=jnp.float32
    )
    summed = lax.psum_scatter(partial, "tensor", scatter_dimension=1, tiled=True)
    projected = (summed * scale[:, None]).astype(jnp.bfloat16)
    return projected.reshape(slot_count, block_len, -1)


def per_device(hidden_in, norm_gain, w_qkv, w_out, home_count, helper_start, segment_ids):
    group_size = lax.axis_size("group")
    tensor_size = lax.axis_size("tensor")
    own_group = lax.axis_index("group")
    own_rank = lax.axis_index("tensor")
    slot_count, block_len, features = hidden_in.shape
    capacity = min(8, group_size - 2)
    local_blocks = capacity // tensor_size
    first_helper = helper_start[0]
    ends = jnp.cumsum(home_count)
    begins = ends - home_count
    groups_iota = jnp.arange(group_size, dtype=jnp.int32)
    send_slot = (groups_iota - first_helper - begins[own_group]) % group_size
    recv_slot = (own_group - first_helper - begins) % group_size
    recv_live = recv_slot < home_count
    placed = (begins + recv_slot) // group_size
    chosen = recv_live[None, :] & (
        placed[None, :] == jnp.arange(capacity, dtype=jnp.int32)[:, None]
    )
    source_of = jnp.sum(jnp.where(chosen, groups_iota[None, :], 0), axis=1)
    home_live = jnp.arange(slot_count, dtype=jnp.int32) < home_count[own_group]
    segments = lax.dynamic_slice_in_dim(segment_ids, own_group * slot_count, slot_count, 0)
    part_rows = w_out.shape[0] // tensor_size
    own_part = lax.dynamic_slice_in_dim(w_out, own_rank * part_rows, part_rows, 0)
    by_kernel = (lax.axis_size("replica"), group_size, tensor_size) == (2, 8, 2)
    projected = project(
        hidden_in, norm_gain, w_qkv, by_kernel, group_size, tensor_size
    )
    by_head = projected.reshape(slot_count, block_len, -1, Q_PER + 2, HD)
    cache = by_head[:, :, :, Q_PER:].reshape(slot_count, block_len, -1)
    kv_cache = jnp.where(home_live[:, None, None], cache, jnp.zeros_like(cache))
    slots = jnp.minimum(send_slot, slot_count - 1)
    if by_kernel:
        positions = jnp.arange(block_len)
        allowed = (positions[:, None] >= positions[None, :])[None] & (
            segments[:, :, None] == segments[:, None, :]
        )
        bias = jnp.where(allowed, 0.0, -jnp.inf).astype(jnp.float32)
        sources = lax.dynamic_slice_in_dim(source_of, own_rank * local_blocks, local_blocks)
        mixed = attend_and_mix(
            slots, sources, projected, bias, own_part, group_size, tensor_size
        )
        return (mixed.reshape(local_blocks, block_len, -1), kv_cache)
    out_part = lax.all_gather(own_part, "group", axis=1, tiled=True)
    out_full = lax.all_gather(out_part, "tensor", axis=0, tiled=True)
    context = attend(by_head, segments).reshape(slot_count, block_len, -1)
    outgoing = jnp.take(context, slots, axis=0)
    arrived = lax.all_to_all(outgoing, "group", split_axis=0, concat_axis=0, tiled=True)
    helped = jnp.take(arrived, source_of, axis=0)
    rows = lax.all_to_all(helped, "tensor", split_axis=0, concat_axis=2, tiled=True)
    mixed = jnp.dot(
        rows.reshape(local_blocks * block_len, -1),
        out_full,
        preferred_element_type=jnp.float32,
    )
    layer_out = mixed.astype(jnp.bfloat16).reshape(local_blocks, block_len, -1)
    return (layer_out, kv_cache)


def solution(mesh):
    in_specs = (
        P(("replica", "group"), None, "tensor"),
        P("tensor"),
        P("group", "tensor"),
        P(None, "group"),
        P("replica"),
        P("replica"),
        P("replica", None),
    )
    out_specs = (
        P(("replica", "group", "tensor"), None, None),
        P(("replica", "group"), None, "tensor"),
    )
    return jax.shard_map(
        per_device, mesh=mesh, in_specs=in_specs, out_specs=out_specs, check_vma=False
    )
```

```python
import functools
import jax
import jax.numpy as jnp
from jax import lax
from jax.experimental import pallas as pl
from jax.experimental.pallas import tpu as pltpu
from jax.sharding import PartitionSpec as P

HD = 128
Q_PER = 4


epsilon = 1e-05


def attend(projected, segments):
    block_len = projected.shape[1]
    queries = projected[:, :, :, :Q_PER]
    keys_part = projected[:, :, :, Q_PER]
    values_part = projected[:, :, :, Q_PER + 1]
    scores = jnp.einsum(
        "bihqd,bjhd->bhqij", queries, keys_part, preferred_element_type=jnp.float32
    ) * HD ** (-0.5)
    positions = jnp.arange(block_len)
    causal = positions[:, None] >= positions[None, :]
    allowed = causal[None] & (segments[:, :, None] == segments[:, None, :])
    scores = jnp.where(allowed[:, None, None], scores, -jnp.inf)
    highest = jnp.max(scores, axis=-1, keepdims=True)
    raised = jnp.exp(scores - highest)
    weights = (raised / jnp.sum(raised, axis=-1, keepdims=True)).astype(jnp.bfloat16)
    context = jnp.einsum(
        "bhqij,bjhd->bihqd", weights, values_part, preferred_element_type=jnp.float32
    )
    return context.astype(jnp.bfloat16).reshape(projected.shape[0] * block_len, -1)


def row_scale(floats, model_width):
    partial_sq = jnp.sum(floats * floats, axis=-1)
    summed = lax.psum(partial_sq, "tensor")
    return lax.rsqrt(summed / model_width + epsilon)


class Spread:
    def __init__(self, line, shard, rows, place, sems, local_sem, sibling_copies):
        self.line, self.shard, self.place = line, shard, place
        self.send_sem, self.recv_sem, self.local_sem = *sems, local_sem
        self.half, self.quarter = rows // 2, rows // 4
        self.rows, self.sibling_copies = rows, sibling_copies
        self.pool = lax.axis_index("replica")
        group, self.core = lax.axis_index("group"), lax.axis_index("tensor")
        self.group, self.z, self.y = group, group // 2, group % 2
        self.across = (1 - self.pool, group, self.core)
        self.beside = (self.pool, self.z * 2 + (1 - self.y), self.core)
        self.sibling = (self.pool, group, 1 - self.core)
        self.count, self.all, self.kin = 0, [], []

    def along(self, step, y):
        return (self.z + step) % self.line * 2 + y

    def peers(self):
        spread = [(self.pool, self.along(d, self.y), self.core) for d in range(1, self.line)]
        return spread + [self.across, self.beside]

    def send(self, src, dst, peer):
        copy = pltpu.make_async_remote_copy(
            src_ref=src,
            dst_ref=dst,
            send_sem=self.send_sem.at[self.count],
            recv_sem=self.recv_sem.at[self.count],
            device_id=peer,
            device_id_type=pl.DeviceIdType.MESH,
        )
        self.count += 1
        copy.start()
        self.all.append(copy)
        return copy

    def relay(self, source, begin, count, peer):
        place = self.place(source, begin, count)
        return self.send(place, place, peer)

    def share(self, source, begin, count):
        if self.sibling_copies:
            self.kin.append(self.relay(source, begin, count, self.sibling))

    def start(self):
        mine = self.pool * self.half
        src = self.shard.at[pl.ds(mine, self.half)]
        dst = self.place(self.group, mine, self.half)
        self.own = pltpu.make_async_copy(
            self.shard, self.place(self.group, 0, self.rows), self.local_sem
        )
        self.own.start()
        self.first = [
            self.send(src, dst, (self.pool, self.along(d, self.y), self.core))
            for d in range(1, self.line)
        ]
        self.sideways = [self.send(src, dst, self.beside)]
        if self.sibling_copies:
            whole = self.place(self.group, 0, self.rows)
            self.kin.append(self.send(self.shard, whole, self.sibling))

    def trade(self):
        mine = self.pool * self.half
        self.over = []
        for d in range(1, self.line):
            self.first[d - 1].wait_recv()
            source = self.along(self.line - d, self.y)
            self.over.append(self.relay(source, mine, self.half, self.across))
            self.sideways.append(self.relay(source, mine, self.half, self.beside))
            self.share(source, mine, self.half)

    def finish(self):
        mine, other = self.pool * self.half, (1 - self.pool) * self.half
        second, third = [], []
        for d in range(self.line):
            self.sideways[d].wait_recv()
            source = self.along(self.line - d, 1 - self.y)
            skip = 0 if d == 0 else self.quarter
            second.append(self.relay(source, mine + skip, self.half - skip, self.across))
            self.share(source, mine, self.half)
            if d > 0:
                self.over[d - 1].wait_recv()
                source = self.along(self.line - d, self.y)
                third.append(self.relay(source, other, self.quarter, self.beside))
                self.share(source, other, self.half)
        self.second, self.third = second, third

    def end(self, arrived=None):
        other = (1 - self.pool) * self.half
        for d in range(self.line):
            skip = 0 if d == 0 else self.quarter
            source = self.along(self.line - d, 1 - self.y)
            self.second[d].wait_recv()
            self.share(source, other + skip, self.half - skip)
            if d > 0:
                self.third[d - 1].wait_recv()
                self.share(source, other, self.quarter)
            if d == 0:
                self.own.wait()
            if arrived is not None:
                arrived((self.z + self.line - d) % self.line)
        for copy in self.kin:
            copy.wait_recv()
        for copy in self.all:
            copy.wait_send()


def copy_counts(line):
    return 5 * line - 3, 10 * line - 5


def greet(peers):
    barrier = pltpu.get_barrier_semaphore()
    for peer in peers:
        pl.semaphore_signal(barrier, inc=1, device_id=peer, device_id_type=pl.DeviceIdType.MESH)
    pl.semaphore_wait(barrier, len(peers))


def project_kernel(
    line, model_width, hidden_ref, gain_ref, rows_ref, out_ref,
    rows_full, kept, sent, got, scaled_ref, squares, own_sem, rsend, rrecv, hsend, hrecv,
    qsend, qrecv,
):
    def place_rows(source, begin, count):
        return rows_full.at[source, pl.ds(begin, count)]

    core = lax.axis_index("tensor")
    spread = Spread(
        line, rows_ref, rows_ref.shape[0], place_rows, (rsend, rrecv), own_sem, False
    )
    per_core = kept.shape[0]
    tokens, width = kept.shape[1:]
    step = 256

    def head_copy(index):
        return pltpu.make_async_remote_copy(
            src_ref=sent.at[index],
            dst_ref=got.at[index],
            send_sem=hsend.at[index],
            recv_sem=hrecv.at[index],
            device_id=spread.sibling,
            device_id_type=pl.DeviceIdType.MESH,
        )

    def multiply(pair, target):
        weights = rows_full[pl.ds(pair * 2, 2)].reshape(width, -1)

        def tile(index, carry):
            rows = pl.ds(pl.multiple_of(index * step, step), step)
            target[pair % per_core, rows] = lax.dot_general(
                scaled_ref[rows],
                weights,
                (((1,), (1,)), ((), ())),
                preferred_element_type=jnp.float32,
            )
            return carry

        lax.fori_loop(0, tokens // step, tile, 0)

    def arrived(pair):
        @pl.when(pair // per_core == core)
        def _():
            multiply(pair, kept)

        @pl.when(pair // per_core != core)
        def _():
            multiply(pair, sent)
            head_copy(pair % per_core).start()

    def prepare(index, carry):
        rows = pl.ds(pl.multiple_of(index * 64, 64), 64)
        floats = hidden_ref[rows].astype(jnp.float32)
        scaled_ref[rows] = (floats * gain_ref[...]).astype(jnp.bfloat16)
        partial_sq = jnp.sum(floats * floats, axis=-1, keepdims=True)
        squares[0, rows] = jnp.broadcast_to(partial_sq, (64, squares.shape[2]))
        return carry

    greet(spread.peers() + [spread.sibling])
    spread.start()
    lax.fori_loop(0, tokens // 64, prepare, 0)
    square_copy = pltpu.make_async_remote_copy(
        src_ref=squares.at[0],
        dst_ref=squares.at[1],
        send_sem=qsend,
        recv_sem=qrecv,
        device_id=spread.sibling,
        device_id_type=pl.DeviceIdType.MESH,
    )
    square_copy.start()
    spread.trade()
    spread.finish()
    spread.end(arrived)
    square_copy.wait()
    scale = lax.rsqrt((squares[0, :, :1] + squares[1, :, :1]) / model_width + epsilon)
    for j in range(per_core):
        head_copy(j).wait()
        total = (kept[j] + got[j]) * scale
        out_ref[:, j * width : (j + 1) * width] = total.astype(jnp.bfloat16)


def project_rows(hidden, gain, rows, group_size, tensor_size, collective_id):
    line = group_size // 2
    few, _ = copy_counts(line)
    tokens, features = hidden.shape
    per_core, width = line // tensor_size, 2 * rows.shape[0]
    vmem = pl.BlockSpec(memory_space=pltpu.VMEM)
    halves = pltpu.VMEM((per_core, tokens, width), jnp.float32)
    return pl.pallas_call(
        functools.partial(project_kernel, line, features * tensor_size),
        out_shape=jax.ShapeDtypeStruct((tokens, per_core * width), jnp.bfloat16),
        in_specs=[vmem, vmem, pl.BlockSpec(memory_space=pl.ANY)],
        out_specs=vmem,
        scratch_shapes=[
            pltpu.VMEM((group_size,) + rows.shape, rows.dtype),
            halves,
            halves,
            halves,
            pltpu.VMEM((tokens, features), jnp.bfloat16),
            pltpu.VMEM((2, tokens, HD), jnp.float32),
            pltpu.SemaphoreType.DMA,
            pltpu.SemaphoreType.DMA((few,)),
            pltpu.SemaphoreType.DMA((few,)),
            pltpu.SemaphoreType.DMA((per_core,)),
            pltpu.SemaphoreType.DMA((per_core,)),
            pltpu.SemaphoreType.DMA,
            pltpu.SemaphoreType.DMA,
        ],
        compiler_params=pltpu.CompilerParams(
            collective_id=collective_id, has_side_effects=True, vmem_limit_bytes=48 * 2**20
        ),
    )(hidden, gain, rows)


def attend_one(projected, bias):
    block_len = projected.shape[0]
    heads = [projected[:, i * HD : (i + 1) * HD] for i in range(Q_PER + 2)]
    queries = jnp.concatenate(heads[:Q_PER], axis=0)
    scores = lax.dot_general(
        queries, heads[Q_PER], (((1,), (1,)), ((), ())), preferred_element_type=jnp.float32
    ) * HD ** (-0.5)
    scores = scores.reshape(Q_PER, block_len, block_len) + bias[None]
    raised = jnp.exp(scores - jnp.max(scores, axis=-1, keepdims=True))
    weights = (raised / jnp.sum(raised, axis=-1, keepdims=True)).astype(jnp.bfloat16)
    context = jnp.dot(
        weights.reshape(Q_PER * block_len, block_len),
        heads[Q_PER + 1],
        preferred_element_type=jnp.float32,
    ).astype(jnp.bfloat16)
    parts = [context[i * block_len : (i + 1) * block_len] for i in range(Q_PER)]
    return jnp.concatenate(parts, axis=1)


def tail_kernel(
    line, slots_ref, source_ref, proj_ref, bias_ref, cols_ref, out_ref,
    w_full, made, got, rows_buf,
    own_sem, csend, crecv, bsend, brecv, ksend, krecv,
):
    groups = 2 * line
    pool, group = lax.axis_index("replica"), lax.axis_index("group")
    core = lax.axis_index("tensor")
    part, width = cols_ref.shape

    def place_cols(source, begin, count):
        top = pl.multiple_of(core * part + begin, part // 4)
        left = pl.multiple_of(source * width, width)
        return w_full.at[pl.ds(top, count), pl.ds(left, width)]

    spread = Spread(line, cols_ref, part, place_cols, (csend, crecv), own_sem, True)

    def block_copy(step):
        return pltpu.make_async_remote_copy(
            src_ref=made.at[step],
            dst_ref=got.at[group, core],
            send_sem=bsend.at[step],
            recv_sem=brecv.at[step],
            device_id=(pool, (group + step) % groups, core),
            device_id_type=pl.DeviceIdType.MESH,
        )

    def kin_copy(step):
        place = got.at[(group + groups - step) % groups, core]
        return pltpu.make_async_remote_copy(
            src_ref=place,
            dst_ref=place,
            send_sem=ksend.at[step],
            recv_sem=krecv.at[step],
            device_id=(pool, group, 1 - core),
            device_id_type=pl.DeviceIdType.MESH,
        )

    others = [(pool, (group + d) % groups, core) for d in range(1, groups)]
    greet(others + [spread.across, spread.sibling])
    spread.start()

    def attend_and_send(step, carry):
        slot = slots_ref[(group + step) % groups]
        made[step] = attend_one(proj_ref[slot], bias_ref[slot])
        block_copy(step).start()
        return carry

    lax.fori_loop(1, groups, attend_and_send, 0)
    slot = slots_ref[group]
    got[group, core] = attend_one(proj_ref[slot], bias_ref[slot])
    kin_copy(0).start()
    spread.trade()
    spread.finish()

    def pass_on(step, carry):
        block_copy(step).wait_recv()
        kin_copy(step).start()
        return carry

    lax.fori_loop(1, groups, pass_on, 0)
    spread.end()

    def settle(step, carry):
        kin_copy(step).wait()
        return carry

    def settle_sent(step, carry):
        block_copy(step).wait_send()
        return carry

    lax.fori_loop(0, groups, settle, 0)
    lax.fori_loop(1, groups, settle_sent, 0)
    block_len, wide = made.shape[1:]
    for b in range(out_ref.shape[0] // block_len):
        block = got[source_ref[b]]
        for c in range(got.shape[1]):
            rows_buf[b * block_len : (b + 1) * block_len, c * wide : (c + 1) * wide] = block[c]

    def column_tile(tile, carry):
        columns = pl.ds(pl.multiple_of(tile * width, width), width)
        out_ref[:, columns] = jnp.dot(
            rows_buf[...], w_full[:, columns], preferred_element_type=jnp.float32
        ).astype(jnp.bfloat16)
        return carry

    lax.fori_loop(0, groups, column_tile, 0)


def attend_and_mix(slots, sources, projected, bias, cols, group_size, tensor_size):
    line = group_size // 2
    _, many = copy_counts(line)
    block_len = projected.shape[1]
    wide = Q_PER * HD
    depth, model_width = tensor_size * cols.shape[0], group_size * cols.shape[1]
    tokens = sources.shape[0] * block_len
    smem, vmem = (pl.BlockSpec(memory_space=m) for m in (pltpu.SMEM, pltpu.VMEM))
    return pl.pallas_call(
        functools.partial(tail_kernel, line),
        out_shape=jax.ShapeDtypeStruct((tokens, model_width), jnp.bfloat16),
        in_specs=[smem, smem, vmem, vmem, pl.BlockSpec(memory_space=pl.ANY)],
        out_specs=vmem,
        scratch_shapes=[
            pltpu.VMEM((depth, model_width), jnp.bfloat16),
            pltpu.VMEM((group_size, block_len, wide), jnp.bfloat16),
            pltpu.VMEM((group_size, tensor_size, block_len, wide), jnp.bfloat16),
            pltpu.VMEM((tokens, tensor_size * wide), jnp.bfloat16),
            pltpu.SemaphoreType.DMA,
            pltpu.SemaphoreType.DMA((many,)),
            pltpu.SemaphoreType.DMA((many,)),
        ]
        + [pltpu.SemaphoreType.DMA((group_size,))] * 4,
        compiler_params=pltpu.CompilerParams(
            collective_id=1, has_side_effects=True, vmem_limit_bytes=48 * 2**20
        ),
    )(slots, sources, projected, bias, cols)


def project(hidden_in, norm_gain, w_qkv, by_kernel, group_size, tensor_size):
    slot_count, block_len, features = hidden_in.shape
    if by_kernel:
        flat = hidden_in.reshape(-1, features)
        projected = project_rows(
            flat, norm_gain[None], w_qkv, group_size, tensor_size, 0
        )
        return projected.reshape(slot_count, block_len, -1)
    floats = hidden_in.astype(jnp.float32)
    scale = row_scale(floats, features * tensor_size).reshape(-1)
    scaled = (floats * norm_gain).astype(jnp.bfloat16).reshape(-1, features)
    rows_full = lax.all_gather(w_qkv, "group", axis=0, tiled=True)
    contract = (((1,), (1,)), ((), ()))
    partial = lax.dot_general(
        scaled, rows_full, contract, preferred_element_type=jnp.float32
    )
    summed = lax.psum_scatter(partial, "tensor", scatter_dimension=1, tiled=True)
    projected = (summed * scale[:, None]).astype(jnp.bfloat16)
    return projected.reshape(slot_count, block_len, -1)


def per_device(hidden_in, norm_gain, w_qkv, w_out, home_count, helper_start, segment_ids):
    group_size = lax.axis_size("group")
    tensor_size = lax.axis_size("tensor")
    own_group = lax.axis_index("group")
    own_rank = lax.axis_index("tensor")
    slot_count, block_len, features = hidden_in.shape
    capacity = min(8, group_size - 2)
    local_blocks = capacity // tensor_size
    first_helper = helper_start[0]
    ends = jnp.cumsum(home_count)
    begins = ends - home_count
    groups_iota = jnp.arange(group_size, dtype=jnp.int32)
    send_slot = (groups_iota - first_helper - begins[own_group]) % group_size
    recv_slot = (own_group - first_helper - begins) % group_size
    recv_live = recv_slot < home_count
    placed = (begins + recv_slot) // group_size
    chosen = recv_live[None, :] & (
        placed[None, :] == jnp.arange(capacity, dtype=jnp.int32)[:, None]
    )
    source_of = jnp.sum(jnp.where(chosen, groups_iota[None, :], 0), axis=1)
    home_live = jnp.arange(slot_count, dtype=jnp.int32) < home_count[own_group]
    segments = lax.dynamic_slice_in_dim(segment_ids, own_group * slot_count, slot_count, 0)
    part_rows = w_out.shape[0] // tensor_size
    own_part = lax.dynamic_slice_in_dim(w_out, own_rank * part_rows, part_rows, 0)
    by_kernel = (lax.axis_size("replica"), group_size, tensor_size) == (2, 8, 2)
    projected = project(
        hidden_in, norm_gain, w_qkv, by_kernel, group_size, tensor_size
    )
    by_head = projected.reshape(slot_count, block_len, -1, Q_PER + 2, HD)
    cache = by_head[:, :, :, Q_PER:].reshape(slot_count, block_len, -1)
    kv_cache = jnp.where(home_live[:, None, None], cache, jnp.zeros_like(cache))
    slots = jnp.minimum(send_slot, slot_count - 1)
    if by_kernel:
        positions = jnp.arange(block_len)
        allowed = (positions[:, None] >= positions[None, :])[None] & (
            segments[:, :, None] == segments[:, None, :]
        )
        bias = jnp.where(allowed, 0.0, -jnp.inf).astype(jnp.float32)
        sources = lax.dynamic_slice_in_dim(source_of, own_rank * local_blocks, local_blocks)
        mixed = attend_and_mix(
            slots, sources, projected, bias, own_part, group_size, tensor_size
        )
        return (mixed.reshape(local_blocks, block_len, -1), kv_cache)
    out_part = lax.all_gather(own_part, "group", axis=1, tiled=True)
    out_full = lax.all_gather(out_part, "tensor", axis=0, tiled=True)
    context = attend(by_head, segments).reshape(slot_count, block_len, -1)
    outgoing = jnp.take(context, slots, axis=0)
    arrived = lax.all_to_all(outgoing, "group", split_axis=0, concat_axis=0, tiled=True)
    helped = jnp.take(arrived, source_of, axis=0)
    rows = lax.all_to_all(helped, "tensor", split_axis=0, concat_axis=2, tiled=True)
    mixed = jnp.dot(
        rows.reshape(local_blocks * block_len, -1),
        out_full,
        preferred_element_type=jnp.float32,
    )
    layer_out = mixed.astype(jnp.bfloat16).reshape(local_blocks, block_len, -1)
    return (layer_out, kv_cache)


def solution(mesh):
    in_specs = (
        P(("replica", "group"), None, "tensor"),
        P("tensor"),
        P("group", "tensor"),
        P(None, "group"),
        P("replica"),
        P("replica"),
        P("replica", None),
    )
    out_specs = (
        P(("replica", "group", "tensor"), None, None),
        P(("replica", "group"), None, "tensor"),
    )
    return jax.shard_map(
        per_device, mesh=mesh, in_specs=in_specs, out_specs=out_specs, check_vma=False
    )
```

```python
import functools
import jax
import jax.numpy as jnp
from jax import lax
from jax.experimental import pallas as pl
from jax.experimental.pallas import tpu as pltpu
from jax.sharding import PartitionSpec as P

HD = 128
Q_PER = 4


epsilon = 1e-05


def attend(projected, segments):
    block_len = projected.shape[1]
    queries = projected[:, :, :, :Q_PER]
    keys_part = projected[:, :, :, Q_PER]
    values_part = projected[:, :, :, Q_PER + 1]
    scores = jnp.einsum(
        "bihqd,bjhd->bhqij", queries, keys_part, preferred_element_type=jnp.float32
    ) * HD ** (-0.5)
    positions = jnp.arange(block_len)
    causal = positions[:, None] >= positions[None, :]
    allowed = causal[None] & (segments[:, :, None] == segments[:, None, :])
    scores = jnp.where(allowed[:, None, None], scores, -jnp.inf)
    highest = jnp.max(scores, axis=-1, keepdims=True)
    raised = jnp.exp(scores - highest)
    weights = (raised / jnp.sum(raised, axis=-1, keepdims=True)).astype(jnp.bfloat16)
    context = jnp.einsum(
        "bhqij,bjhd->bihqd", weights, values_part, preferred_element_type=jnp.float32
    )
    return context.astype(jnp.bfloat16).reshape(projected.shape[0] * block_len, -1)


def row_scale(floats, model_width):
    partial_sq = jnp.sum(floats * floats, axis=-1)
    summed = lax.psum(partial_sq, "tensor")
    return lax.rsqrt(summed / model_width + epsilon)


class Spread:
    def __init__(self, line, shard, rows, place, sems, local_sem, sibling_copies):
        self.line, self.shard, self.place = line, shard, place
        self.send_sem, self.recv_sem, self.local_sem = *sems, local_sem
        self.half, self.quarter = rows // 2, rows // 4
        self.rows, self.sibling_copies = rows, sibling_copies
        self.pool = lax.axis_index("replica")
        group, self.core = lax.axis_index("group"), lax.axis_index("tensor")
        self.group, self.z, self.y = group, group // 2, group % 2
        self.across = (1 - self.pool, group, self.core)
        self.beside = (self.pool, self.z * 2 + (1 - self.y), self.core)
        self.sibling = (self.pool, group, 1 - self.core)
        self.count, self.all, self.kin = 0, [], []

    def along(self, step, y):
        return (self.z + step) % self.line * 2 + y

    def peers(self):
        spread = [(self.pool, self.along(d, self.y), self.core) for d in range(1, self.line)]
        return spread + [self.across, self.beside]

    def send(self, src, dst, peer):
        copy = pltpu.make_async_remote_copy(
            src_ref=src,
            dst_ref=dst,
            send_sem=self.send_sem.at[self.count],
            recv_sem=self.recv_sem.at[self.count],
            device_id=peer,
            device_id_type=pl.DeviceIdType.MESH,
        )
        self.count += 1
        copy.start()
        self.all.append(copy)
        return copy

    def relay(self, source, begin, count, peer):
        place = self.place(source, begin, count)
        return self.send(place, place, peer)

    def share(self, source, begin, count):
        if self.sibling_copies:
            self.kin.append(self.relay(source, begin, count, self.sibling))

    def start(self):
        mine = self.pool * self.half
        src = self.shard.at[pl.ds(mine, self.half)]
        dst = self.place(self.group, mine, self.half)
        self.own = pltpu.make_async_copy(
            self.shard, self.place(self.group, 0, self.rows), self.local_sem
        )
        self.own.start()
        self.first = [
            self.send(src, dst, (self.pool, self.along(d, self.y), self.core))
            for d in range(1, self.line)
        ]
        self.sideways = [self.send(src, dst, self.beside)]
        if self.sibling_copies:
            whole = self.place(self.group, 0, self.rows)
            self.kin.append(self.send(self.shard, whole, self.sibling))

    def trade(self):
        mine = self.pool * self.half
        self.over = []
        for d in range(1, self.line):
            self.first[d - 1].wait_recv()
            source = self.along(self.line - d, self.y)
            self.over.append(self.relay(source, mine, self.half, self.across))
            self.sideways.append(self.relay(source, mine, self.half, self.beside))
            self.share(source, mine, self.half)

    def finish(self):
        mine, other = self.pool * self.half, (1 - self.pool) * self.half
        second, third = [], []
        for d in range(self.line):
            self.sideways[d].wait_recv()
            source = self.along(self.line - d, 1 - self.y)
            skip = 0 if d == 0 else self.quarter
            second.append(self.relay(source, mine + skip, self.half - skip, self.across))
            self.share(source, mine, self.half)
            if d > 0:
                self.over[d - 1].wait_recv()
                source = self.along(self.line - d, self.y)
                third.append(self.relay(source, other, self.quarter, self.beside))
                self.share(source, other, self.half)
        self.second, self.third = second, third

    def end(self, arrived=None):
        other = (1 - self.pool) * self.half
        for d in range(self.line):
            skip = 0 if d == 0 else self.quarter
            source = self.along(self.line - d, 1 - self.y)
            self.second[d].wait_recv()
            self.share(source, other + skip, self.half - skip)
            if d > 0:
                self.third[d - 1].wait_recv()
                self.share(source, other, self.quarter)
            if d == 0:
                self.own.wait()
            if arrived is not None:
                arrived((self.z + self.line - d) % self.line)
        for copy in self.kin:
            copy.wait_recv()
        for copy in self.all:
            copy.wait_send()


def copy_counts(line):
    return 5 * line - 3, 10 * line - 5


def greet(peers):
    barrier = pltpu.get_barrier_semaphore()
    for peer in peers:
        pl.semaphore_signal(barrier, inc=1, device_id=peer, device_id_type=pl.DeviceIdType.MESH)
    pl.semaphore_wait(barrier, len(peers))


def project_kernel(
    line, model_width, hidden_ref, gain_ref, rows_ref, out_ref,
    rows_full, kept, sent, got, scaled_ref, squares, own_sem, rsend, rrecv, hsend, hrecv,
    qsend, qrecv,
):
    def place_rows(source, begin, count):
        return rows_full.at[source, pl.ds(begin, count)]

    core = lax.axis_index("tensor")
    spread = Spread(
        line, rows_ref, rows_ref.shape[0], place_rows, (rsend, rrecv), own_sem, False
    )
    per_core = kept.shape[0]
    tokens, width = kept.shape[1:]
    step = 256

    def head_copy(index):
        return pltpu.make_async_remote_copy(
            src_ref=sent.at[index],
            dst_ref=got.at[index],
            send_sem=hsend.at[index],
            recv_sem=hrecv.at[index],
            device_id=spread.sibling,
            device_id_type=pl.DeviceIdType.MESH,
        )

    def multiply(pair, target):
        weights = rows_full[pl.ds(pair * 2, 2)].reshape(width, -1)

        def tile(index, carry):
            rows = pl.ds(pl.multiple_of(index * step, step), step)
            target[pair % per_core, rows] = lax.dot_general(
                scaled_ref[rows],
                weights,
                (((1,), (1,)), ((), ())),
                preferred_element_type=jnp.float32,
            )
            return carry

        lax.fori_loop(0, tokens // step, tile, 0)

    def arrived(pair):
        @pl.when(pair // per_core == core)
        def _():
            multiply(pair, kept)

        @pl.when(pair // per_core != core)
        def _():
            multiply(pair, sent)
            head_copy(pair % per_core).start()

    def prepare(index, carry):
        rows = pl.ds(pl.multiple_of(index * 64, 64), 64)
        floats = hidden_ref[rows].astype(jnp.float32)
        scaled_ref[rows] = (floats * gain_ref[...]).astype(jnp.bfloat16)
        partial_sq = jnp.sum(floats * floats, axis=-1, keepdims=True)
        squares[0, rows] = jnp.broadcast_to(partial_sq, (64, squares.shape[2]))
        return carry

    greet(spread.peers() + [spread.sibling])
    spread.start()
    lax.fori_loop(0, tokens // 64, prepare, 0)
    square_copy = pltpu.make_async_remote_copy(
        src_ref=squares.at[0],
        dst_ref=squares.at[1],
        send_sem=qsend,
        recv_sem=qrecv,
        device_id=spread.sibling,
        device_id_type=pl.DeviceIdType.MESH,
    )
    square_copy.start()
    spread.trade()
    spread.finish()
    spread.end(arrived)
    square_copy.wait()
    scale = lax.rsqrt((squares[0, :, :1] + squares[1, :, :1]) / model_width + epsilon)
    for j in range(per_core):
        head_copy(j).wait()
        total = (kept[j] + got[j]) * scale
        out_ref[:, j * width : (j + 1) * width] = total.astype(jnp.bfloat16)


def project_rows(hidden, gain, rows, group_size, tensor_size, collective_id):
    line = group_size // 2
    few, _ = copy_counts(line)
    tokens, features = hidden.shape
    per_core, width = line // tensor_size, 2 * rows.shape[0]
    vmem = pl.BlockSpec(memory_space=pltpu.VMEM)
    halves = pltpu.VMEM((per_core, tokens, width), jnp.float32)
    return pl.pallas_call(
        functools.partial(project_kernel, line, features * tensor_size),
        out_shape=jax.ShapeDtypeStruct((tokens, per_core * width), jnp.bfloat16),
        in_specs=[vmem, vmem, pl.BlockSpec(memory_space=pl.ANY)],
        out_specs=vmem,
        scratch_shapes=[
            pltpu.VMEM((group_size,) + rows.shape, rows.dtype),
            halves,
            halves,
            halves,
            pltpu.VMEM((tokens, features), jnp.bfloat16),
            pltpu.VMEM((2, tokens, HD), jnp.float32),
            pltpu.SemaphoreType.DMA,
            pltpu.SemaphoreType.DMA((few,)),
            pltpu.SemaphoreType.DMA((few,)),
            pltpu.SemaphoreType.DMA((per_core,)),
            pltpu.SemaphoreType.DMA((per_core,)),
            pltpu.SemaphoreType.DMA,
            pltpu.SemaphoreType.DMA,
        ],
        compiler_params=pltpu.CompilerParams(
            collective_id=collective_id, has_side_effects=True, vmem_limit_bytes=48 * 2**20
        ),
    )(hidden, gain, rows)


def attend_one(projected, bias):
    block_len = projected.shape[0]
    heads = [projected[:, i * HD : (i + 1) * HD] for i in range(Q_PER + 2)]
    queries = jnp.concatenate(heads[:Q_PER], axis=0)
    scores = lax.dot_general(
        queries, heads[Q_PER], (((1,), (1,)), ((), ())), preferred_element_type=jnp.float32
    ) * HD ** (-0.5)
    scores = scores.reshape(Q_PER, block_len, block_len) + bias[None]
    raised = jnp.exp(scores - jnp.max(scores, axis=-1, keepdims=True))
    weights = (raised / jnp.sum(raised, axis=-1, keepdims=True)).astype(jnp.bfloat16)
    context = jnp.dot(
        weights.reshape(Q_PER * block_len, block_len),
        heads[Q_PER + 1],
        preferred_element_type=jnp.float32,
    ).astype(jnp.bfloat16)
    parts = [context[i * block_len : (i + 1) * block_len] for i in range(Q_PER)]
    return jnp.concatenate(parts, axis=1)


def tail_kernel(
    line, slots_ref, source_ref, proj_ref, bias_ref, cols_ref, out_ref,
    w_full, made, got, rows_buf,
    own_sem, csend, crecv, bsend, brecv, ksend, krecv,
):
    groups = 2 * line
    pool, group = lax.axis_index("replica"), lax.axis_index("group")
    core = lax.axis_index("tensor")
    part, width = cols_ref.shape

    def place_cols(source, begin, count):
        top = pl.multiple_of(core * part + begin, part // 4)
        left = pl.multiple_of(source * width, width)
        return w_full.at[pl.ds(top, count), pl.ds(left, width)]

    spread = Spread(line, cols_ref, part, place_cols, (csend, crecv), own_sem, True)

    def block_copy(step):
        return pltpu.make_async_remote_copy(
            src_ref=made.at[step],
            dst_ref=got.at[group, core],
            send_sem=bsend.at[step],
            recv_sem=brecv.at[step],
            device_id=(pool, (group + step) % groups, core),
            device_id_type=pl.DeviceIdType.MESH,
        )

    def kin_copy(step):
        place = got.at[(group + groups - step) % groups, core]
        return pltpu.make_async_remote_copy(
            src_ref=place,
            dst_ref=place,
            send_sem=ksend.at[step],
            recv_sem=krecv.at[step],
            device_id=(pool, group, 1 - core),
            device_id_type=pl.DeviceIdType.MESH,
        )

    others = [(pool, (group + d) % groups, core) for d in range(1, groups)]
    greet(others + [spread.across, spread.sibling])
    spread.start()

    def attend_and_send(step, carry):
        slot = slots_ref[(group + step) % groups]
        made[step] = attend_one(proj_ref[slot], bias_ref[slot])
        block_copy(step).start()
        return carry

    lax.fori_loop(1, groups, attend_and_send, 0)
    slot = slots_ref[group]
    got[group, core] = attend_one(proj_ref[slot], bias_ref[slot])
    kin_copy(0).start()
    spread.trade()
    spread.finish()

    def pass_on(step, carry):
        block_copy(step).wait_recv()
        kin_copy(step).start()
        return carry

    lax.fori_loop(1, groups, pass_on, 0)
    spread.end()

    def settle(step, carry):
        kin_copy(step).wait()
        return carry

    def settle_sent(step, carry):
        block_copy(step).wait_send()
        return carry

    lax.fori_loop(0, groups, settle, 0)
    lax.fori_loop(1, groups, settle_sent, 0)
    block_len, wide = made.shape[1:]
    for b in range(out_ref.shape[0] // block_len):
        block = got[source_ref[b]]
        for c in range(got.shape[1]):
            rows_buf[b * block_len : (b + 1) * block_len, c * wide : (c + 1) * wide] = block[c]

    def column_tile(tile, carry):
        columns = pl.ds(pl.multiple_of(tile * width, width), width)
        out_ref[:, columns] = jnp.dot(
            rows_buf[...], w_full[:, columns], preferred_element_type=jnp.float32
        ).astype(jnp.bfloat16)
        return carry

    lax.fori_loop(0, groups, column_tile, 0)


def attend_and_mix(slots, sources, projected, bias, cols, group_size, tensor_size):
    line = group_size // 2
    _, many = copy_counts(line)
    block_len = projected.shape[1]
    wide = Q_PER * HD
    depth, model_width = tensor_size * cols.shape[0], group_size * cols.shape[1]
    tokens = sources.shape[0] * block_len
    smem, vmem = (pl.BlockSpec(memory_space=m) for m in (pltpu.SMEM, pltpu.VMEM))
    return pl.pallas_call(
        functools.partial(tail_kernel, line),
        out_shape=jax.ShapeDtypeStruct((tokens, model_width), jnp.bfloat16),
        in_specs=[smem, smem, vmem, vmem, pl.BlockSpec(memory_space=pl.ANY)],
        out_specs=vmem,
        scratch_shapes=[
            pltpu.VMEM((depth, model_width), jnp.bfloat16),
            pltpu.VMEM((group_size, block_len, wide), jnp.bfloat16),
            pltpu.VMEM((group_size, tensor_size, block_len, wide), jnp.bfloat16),
            pltpu.VMEM((tokens, tensor_size * wide), jnp.bfloat16),
            pltpu.SemaphoreType.DMA,
            pltpu.SemaphoreType.DMA((many,)),
            pltpu.SemaphoreType.DMA((many,)),
        ]
        + [pltpu.SemaphoreType.DMA((group_size,))] * 4,
        compiler_params=pltpu.CompilerParams(
            collective_id=1, has_side_effects=True, vmem_limit_bytes=48 * 2**20
        ),
    )(slots, sources, projected, bias, cols)


def project(hidden_in, norm_gain, w_qkv, by_kernel, group_size, tensor_size):
    slot_count, block_len, features = hidden_in.shape
    if by_kernel:
        flat = hidden_in.reshape(-1, features)
        projected = project_rows(
            flat, norm_gain[None], w_qkv, group_size, tensor_size, 0
        )
        return projected.reshape(slot_count, block_len, -1)
    floats = hidden_in.astype(jnp.float32)
    scale = row_scale(floats, features * tensor_size).reshape(-1)
    scaled = (floats * norm_gain).astype(jnp.bfloat16).reshape(-1, features)
    rows_full = lax.all_gather(w_qkv, "group", axis=0, tiled=True)
    contract = (((1,), (1,)), ((), ()))
    partial = lax.dot_general(
        scaled, rows_full, contract, preferred_element_type=jnp.float32
    )
    summed = lax.psum_scatter(partial, "tensor", scatter_dimension=1, tiled=True)
    projected = (summed * scale[:, None]).astype(jnp.bfloat16)
    return projected.reshape(slot_count, block_len, -1)


def per_device(hidden_in, norm_gain, w_qkv, w_out, home_count, helper_start, segment_ids):
    group_size = lax.axis_size("group")
    tensor_size = lax.axis_size("tensor")
    own_group = lax.axis_index("group")
    own_rank = lax.axis_index("tensor")
    slot_count, block_len, features = hidden_in.shape
    capacity = min(8, group_size - 2)
    local_blocks = capacity // tensor_size
    first_helper = helper_start[0]
    ends = jnp.cumsum(home_count)
    begins = ends - home_count
    groups_iota = jnp.arange(group_size, dtype=jnp.int32)
    send_slot = (groups_iota - first_helper - begins[own_group]) % group_size
    recv_slot = (own_group - first_helper - begins) % group_size
    recv_live = recv_slot < home_count
    placed = (begins + recv_slot) // group_size
    chosen = recv_live[None, :] & (
        placed[None, :] == jnp.arange(capacity, dtype=jnp.int32)[:, None]
    )
    source_of = jnp.sum(jnp.where(chosen, groups_iota[None, :], 0), axis=1)
    home_live = jnp.arange(slot_count, dtype=jnp.int32) < home_count[own_group]
    segments = lax.dynamic_slice_in_dim(segment_ids, own_group * slot_count, slot_count, 0)
    part_rows = w_out.shape[0] // tensor_size
    own_part = lax.dynamic_slice_in_dim(w_out, own_rank * part_rows, part_rows, 0)
    by_kernel = (lax.axis_size("replica"), group_size, tensor_size) == (2, 8, 2)
    projected = project(
        hidden_in, norm_gain, w_qkv, by_kernel, group_size, tensor_size
    )
    by_head = projected.reshape(slot_count, block_len, -1, Q_PER + 2, HD)
    if projected.shape[-1] == (Q_PER + 2) * HD:
        cache = projected[:, :, Q_PER * HD :]
    else:
        cache = by_head[:, :, :, Q_PER:].reshape(slot_count, block_len, -1)
    kv_cache = jnp.where(home_live[:, None, None], cache, jnp.zeros_like(cache))
    slots = jnp.minimum(send_slot, slot_count - 1)
    if by_kernel:
        positions = jnp.arange(block_len)
        allowed = (positions[:, None] >= positions[None, :])[None] & (
            segments[:, :, None] == segments[:, None, :]
        )
        bias = jnp.where(allowed, 0.0, -jnp.inf).astype(jnp.float32)
        sources = lax.dynamic_slice_in_dim(source_of, own_rank * local_blocks, local_blocks)
        mixed = attend_and_mix(
            slots, sources, projected, bias, own_part, group_size, tensor_size
        )
        return (mixed.reshape(local_blocks, block_len, -1), kv_cache)
    out_part = lax.all_gather(own_part, "group", axis=1, tiled=True)
    out_full = lax.all_gather(out_part, "tensor", axis=0, tiled=True)
    context = attend(by_head, segments).reshape(slot_count, block_len, -1)
    outgoing = jnp.take(context, slots, axis=0)
    arrived = lax.all_to_all(outgoing, "group", split_axis=0, concat_axis=0, tiled=True)
    helped = jnp.take(arrived, source_of, axis=0)
    rows = lax.all_to_all(helped, "tensor", split_axis=0, concat_axis=2, tiled=True)
    mixed = jnp.dot(
        rows.reshape(local_blocks * block_len, -1),
        out_full,
        preferred_element_type=jnp.float32,
    )
    layer_out = mixed.astype(jnp.bfloat16).reshape(local_blocks, block_len, -1)
    return (layer_out, kv_cache)


def solution(mesh):
    in_specs = (
        P(("replica", "group"), None, "tensor"),
        P("tensor"),
        P("group", "tensor"),
        P(None, "group"),
        P("replica"),
        P("replica"),
        P("replica", None),
    )
    out_specs = (
        P(("replica", "group", "tensor"), None, None),
        P(("replica", "group"), None, "tensor"),
    )
    return jax.shard_map(
        per_device, mesh=mesh, in_specs=in_specs, out_specs=out_specs, check_vma=False
    )
```
